512 devices in a mesh: row: 16 (over z_lo, x), col: 32 (over y, z_hi, core).
Axes of the slice: x: 4, y: 4, z: 16 (z_hi: 4, z_lo: 4; z = z_hi * 4 + z_lo), core: 2. Of those that a mesh axis runs over, the one named last changes fastest.
Arguments:
- pair_rep: bfloat16 [256, 256, 128], P('row', 'col'), may hold values from -6 to 6
- cotangent: bfloat16 [256, 256, 128], P('row', 'col'), may hold values from -6 to 6
- contact: int32 [16, 16, 16], replicated, may hold values 0 or 1
- norm_gain: float32 [128], replicated, may hold values from 0.5 to 1.5
- w_out_proj: bfloat16 [128, 512], replicated, may hold values from -0.5 to 0.5
- w_in_proj: bfloat16 [128, 512], replicated, may hold values from -0.5 to 0.5
- update_gain: float32 [2, 128], replicated, may hold values from 0.5 to 1.5
- w_gate: bfloat16 [128, 256], replicated, may hold values from -0.5 to 0.5
- w_final: bfloat16 [2, 128, 128], replicated, may hold values from -0.5 to 0.5
Outputs:
- updated: bfloat16 [256, 256, 128], P('row', 'col')
- grad_pair: bfloat16 [256, 256, 128], P('row', 'col')
The draws below stay inside these ranges and needn't reach their ends.
All inputs are finite; a program needn't handle non-finite values.
Results may differ from the reference program's by a relative error of at most 0.018.
Values may be sent and summed in bfloat16 or wider, within the bound.
No kernel may reach another device: no remote copies, remote signals or barrier semaphores. Data moves between devices by JAX's collectives and lax.ppermute only.
A program may use at most 128 MiB of HBM per device.

```python
import jax
import jax.numpy as jnp
from jax import lax

CH = 128
BLOCKS = 16
ROW_RES = 16
RES = 256
COL_RES = 8


def touch_ends(values, stream_key, smallest, high):
    place = [jax.random.randint(jax.random.fold_in(stream_key, axis), (), 0, length) for axis, length in enumerate(values.shape)]
    main_axis = values.shape.index(max(values.shape))
    beside = place[:main_axis] + [(place[main_axis] + 1) % values.shape[main_axis]] + place[main_axis + 1:]
    return values.at[tuple(place)].set(smallest).at[tuple(beside)].set(high)


def levels(own_key, extent, split, low, largest):
    level, own = 1.0, jax.random.fold_in(own_key, 6)
    for position, shards_of in split:
        heights = jnp.exp(jax.random.uniform(jax.random.fold_in(own, position), (shards_of,), jnp.float32, low / len(split), largest / len(split)))
        level = level * jnp.repeat(heights, extent[position] // shards_of).reshape([-1 if axis == position else 1 for axis in range(len(extent))])
    return level


def scatter_about(own_key, extent, spread, bound, split=(), kind=jnp.bfloat16):
    entries = spread * jax.random.normal(own_key, extent, jnp.float32)
    if split:
        entries = entries * levels(own_key, extent, split, -0.22, 0.18)
    return jnp.clip(entries, -bound, bound).astype(kind)


def setup_inputs(seed: int = 0) -> dict:
    splits = jax.random.split(jax.random.key(seed), 10)
    pair_rep = scatter_about(splits[0], (RES, RES, CH), 1.0, 6.0, ((0, 16), (1, 32)))
    cotangent = scatter_about(splits[1], (RES, RES, CH), 1.0, 6.0, ((0, 16), (1, 32)))
    contact = touch_ends((jax.random.randint(splits[2], (BLOCKS, BLOCKS, BLOCKS), 0, 2) < 1).astype(jnp.int32), jax.random.fold_in(splits[2], 1), 0, 1)
    norm_gain = jnp.clip(1.0 + 0.1 * jax.random.normal(splits[3], (CH,), jnp.float32), 0.5, 1.5)
    w_out_proj = scatter_about(splits[4], (CH, 4 * CH), CH ** -0.5, 0.5)
    w_in_proj = scatter_about(splits[5], (CH, 4 * CH), CH ** -0.5, 0.5)
    update_gain = jnp.clip(1.0 + 0.1 * jax.random.normal(splits[6], (2, CH), jnp.float32), 0.5, 1.5)
    w_gate = scatter_about(splits[7], (CH, 2 * CH), CH ** -0.5, 0.5)
    w_final = scatter_about(splits[8], (2, CH, CH), CH ** -0.5, 0.5)
    return {"pair_rep": pair_rep, "cotangent": cotangent, "contact": contact, "norm_gain": norm_gain, "w_out_proj": w_out_proj, "w_in_proj": w_in_proj, "update_gain": update_gain, "w_gate": w_gate, "w_final": w_final}


EPSILON = 1e-05

def normalize(values, gain):
    center = lax.optimization_barrier(jnp.mean(values, axis=-1, keepdims=True))
    shifted = values - center
    inverse = lax.rsqrt(lax.optimization_barrier(jnp.mean(shifted * shifted, axis=-1, keepdims=True)) + EPSILON)
    scaled = shifted * inverse
    return (scaled * gain, scaled, inverse)

def normalize_back(upstream, gain, scaled, inverse):
    weighted = upstream * gain
    first_mean = lax.optimization_barrier(jnp.mean(weighted, axis=-1, keepdims=True))
    second_mean = lax.optimization_barrier(jnp.mean(weighted * scaled, axis=-1, keepdims=True))
    return inverse * (weighted - first_mean - scaled * second_mean)

def gated_pairs(projected, channels):
    first = jax.nn.sigmoid(projected[..., 0:channels]) * projected[..., channels:2 * channels]
    second = jax.nn.sigmoid(projected[..., 2 * channels:3 * channels]) * projected[..., 3 * channels:]
    return (first.astype(jnp.bfloat16), second.astype(jnp.bfloat16))

def gated_back(grad_first, grad_second, projected, channels):
    sig_first = jax.nn.sigmoid(projected[..., 0:channels])
    sig_second = jax.nn.sigmoid(projected[..., 2 * channels:3 * channels])
    return jnp.concatenate([grad_first * projected[..., channels:2 * channels] * sig_first * (1.0 - sig_first), grad_first * sig_first, grad_second * projected[..., 3 * channels:] * sig_second * (1.0 - sig_second), grad_second * sig_second], axis=-1)

def contract(left_side, right_side, mask_perm, group, rounded):
    block_width = RES // BLOCKS
    piece_len = min(group, block_width)
    summed = jnp.zeros((left_side.shape[0], right_side.shape[0], CH), jnp.float32)
    for group_first in range(0, RES, group):
        partial_value = jnp.zeros_like(summed)
        for piece_first in range(group_first, group_first + group, piece_len):
            mask_layer = mask_perm[:, :, piece_first // block_width].astype(jnp.float32)
            weights = jnp.repeat(jnp.repeat(mask_layer, block_width, axis=0), block_width, axis=1)
            left_piece = left_side[:, piece_first:piece_first + piece_len].astype(jnp.float32)
            right_piece = right_side[:, piece_first:piece_first + piece_len].astype(jnp.float32)
            partial_value = partial_value + weights[:, :, None] * jnp.einsum('prc,qrc->pqc', left_piece, right_piece)
        if rounded:
            partial_value = lax.optimization_barrier(partial_value.astype(jnp.bfloat16)).astype(jnp.float32)
        summed = summed + partial_value
    return summed

def swap_first(values):
    return jnp.transpose(values, (1, 0, 2))

def reference(pair_rep, cotangent, contact, norm_gain, w_out_proj, w_in_proj, update_gain, w_gate, w_final):
    pair_f32 = pair_rep.astype(jnp.float32)
    normed, scaled_pair, inverse_pair = normalize(pair_f32, norm_gain)
    normed_half = normed.astype(jnp.bfloat16)
    out_proj = jnp.dot(normed_half, w_out_proj, preferred_element_type=jnp.float32)
    in_proj = jnp.dot(normed_half, w_in_proj, preferred_element_type=jnp.float32)
    left_out, right_out = gated_pairs(out_proj, CH)
    left_in, right_in = gated_pairs(in_proj, CH)
    triangle_out = contract(left_out, right_out, contact, RES, False)
    triangle_in = contract(swap_first(left_in), swap_first(right_in), contact, ROW_RES, True)
    normed_out, scaled_out, inverse_out = normalize(triangle_out, update_gain[0])
    normed_in, scaled_in, inverse_in = normalize(triangle_in, update_gain[1])
    norm_out = normed_out.astype(jnp.bfloat16)
    norm_in = normed_in.astype(jnp.bfloat16)
    gate = jax.nn.sigmoid(jnp.dot(normed_half, w_gate, preferred_element_type=jnp.float32))
    final_out = jnp.dot(norm_out, w_final[0], preferred_element_type=jnp.float32)
    final_in = jnp.dot(norm_in, w_final[1], preferred_element_type=jnp.float32)
    updated = (pair_f32 + gate[..., :CH] * final_out + gate[..., CH:] * final_in).astype(jnp.bfloat16)
    upstream = cotangent.astype(jnp.float32)
    grad_final_out = (upstream * gate[..., :CH]).astype(jnp.bfloat16)
    grad_final_in = (upstream * gate[..., CH:]).astype(jnp.bfloat16)
    grad_gate = (jnp.concatenate([upstream * final_out, upstream * final_in], axis=-1) * gate * (1.0 - gate)).astype(jnp.bfloat16)
    grad_norm_out = jnp.dot(grad_final_out, w_final[0].T, preferred_element_type=jnp.float32)
    grad_norm_in = jnp.dot(grad_final_in, w_final[1].T, preferred_element_type=jnp.float32)
    grad_tri_out = normalize_back(grad_norm_out, update_gain[0], scaled_out, inverse_out).astype(jnp.bfloat16)
    grad_tri_in = normalize_back(grad_norm_in, update_gain[1], scaled_in, inverse_in).astype(jnp.bfloat16)
    grad_left_out = contract(grad_tri_out, swap_first(right_out), jnp.transpose(contact, (0, 2, 1)), RES, False)
    grad_right_out = contract(swap_first(grad_tri_out), swap_first(left_out), jnp.transpose(contact, (1, 2, 0)), ROW_RES, True)
    grad_right_in = contract(left_in, swap_first(grad_tri_in), jnp.transpose(contact, (2, 1, 0)), RES, False)
    grad_left_in = contract(right_in, grad_tri_in, jnp.transpose(contact, (2, 0, 1)), COL_RES, True)
    grad_proj_out = gated_back(grad_left_out, grad_right_out, out_proj, CH).astype(jnp.bfloat16)
    grad_proj_in = gated_back(grad_left_in, grad_right_in, in_proj, CH).astype(jnp.bfloat16)
    grad_normed = jnp.dot(grad_proj_out, w_out_proj.T, preferred_element_type=jnp.float32)
    grad_normed = grad_normed + jnp.dot(grad_proj_in, w_in_proj.T, preferred_element_type=jnp.float32)
    grad_normed = grad_normed + jnp.dot(grad_gate, w_gate.T, preferred_element_type=jnp.float32)
    grad_pair = (upstream + normalize_back(grad_normed, norm_gain, scaled_pair, inverse_pair)).astype(jnp.bfloat16)
    return (updated, grad_pair)
```

```python
import jax
import jax.numpy as jnp
from jax import lax
from jax.experimental import pallas as pl
from jax.experimental.pallas import tpu as pltpu
from jax.sharding import PartitionSpec as P


EPSILON = 1e-05
BF = jnp.bfloat16
F32 = jnp.float32


def dot(a, b, dims=((1,), (0,))):
    return lax.dot_general(a, b, (dims, ((), ())), preferred_element_type=F32)


def norm(values):
    center = jnp.mean(values, axis=0, keepdims=True)
    shifted = values - center
    inverse = lax.rsqrt(jnp.mean(shifted * shifted, axis=0, keepdims=True) + EPSILON)
    return shifted * inverse, inverse


def norm_back(weighted, scaled, inverse):
    first = jnp.mean(weighted, axis=0, keepdims=True)
    second = jnp.mean(weighted * scaled, axis=0, keepdims=True)
    return inverse * (weighted - first - scaled * second)


def pair_order():
    here = lax.broadcasted_iota(jnp.int32, (128, 128), 0)
    there = lax.broadcasted_iota(jnp.int32, (128, 128), 1)
    same = (here >> 3 == (there & 15)) & ((here & 7) == there >> 4)
    return same.astype(F32).astype(BF)


def groups(values):
    return values.reshape(16, 8, 128)


def first_kernel(pair, gain, w_out, w_in, w_gate, send, proj, gates, scaled_t, inv):
    pair_t = dot(pair[...], pair_order(), ((0,), (0,)))
    scaled, inverse = norm(pair_t)
    normed = (scaled * gain[...]).astype(BF)
    scaled_t[...] = scaled
    inv[...] = inverse
    for half, weights in enumerate((w_out, w_in)):
        p = dot(weights[...], normed, ((0,), (0,)))
        proj[half] = p
        send[:, 2 * half] = groups(jax.nn.sigmoid(p[0:128]) * p[128:256]).astype(BF)
        send[:, 2 * half + 1] = groups(jax.nn.sigmoid(p[256:384]) * p[384:512]).astype(BF)
    gates[...] = jax.nn.sigmoid(dot(w_gate[...], normed, ((0,), (0,))))


def swap_groups(rows):
    rows = list(rows)
    group = lax.broadcasted_iota(jnp.int32, rows[0].shape, rows[0].ndim - 1) >> 4
    last = rows[0].ndim - 1
    for step in (4, 2, 1):
        low = (group & step) == 0
        for a in range(8):
            if a & step:
                continue
            x, y = rows[a], rows[a + step]
            rows[a] = jnp.where(low, x, pltpu.roll(y, 16 * step, last))
            rows[a + step] = jnp.where(low, pltpu.roll(x, 128 - 16 * step, last), y)
    return rows


def spread_kernel(got, send, held):
    amount = got.shape[1]
    for half in range(2):
        rows = swap_groups(
            [got[8 * half + r].astype(F32).reshape(amount * 8, 128) for r in range(8)]
        )
        for q in range(8):
            for a in range(amount):
                held[:, a, q, 128 * half : 128 * half + 128] = rows[q][8 * a : 8 * a + 8]
    values = held[...].astype(BF)
    for mate in range(4):
        send[:, mate] = values


def collect_kernel(got, send, held, out):
    held[...] = got[...].astype(F32)
    for mate in range(4):
        for tile in range(got.shape[3] // 128):
            rows = swap_groups(
                [held[:, mate, q, 128 * tile : 128 * tile + 128] for q in range(8)]
            )
            for g in range(8):
                out[mate, g & 3, 2 * tile + (g >> 2)] = rows[g]
    send[...] = out[...].astype(BF)


def whole(got, a):
    return got[:, a].astype(F32).reshape(256, 256).astype(BF)


def block_table():
    place = lax.broadcasted_iota(jnp.int32, (256, 16), 0) >> 4
    label = lax.broadcasted_iota(jnp.int32, (256, 16), 1)
    return (place == label).astype(F32).astype(BF)


def masked(values, table, layer, flip):
    side = dot(table, layer, ((1,), (1 if flip else 0,))).astype(BF)
    return values * dot(side, table, ((1,), (1,))).astype(BF)


def quarter(values, mate):
    place = lax.broadcasted_iota(jnp.int32, (64, 256), 0) + 64 * mate
    label = lax.broadcasted_iota(jnp.int32, (64, 256), 1)
    return dot((place == label).astype(F32).astype(BF), values, ((1,), (1,))).astype(BF)


def own_rows(got, a, mate):
    return got[pl.ds(8 * mate, 8), a].astype(F32).reshape(64, 256).astype(BF)


NN = ((1,), (0,))
NT = ((1,), (1,))


def forward_kernel(spot, got, by_i, send):
    mate = spot[0]
    table = block_table()
    right_out, right_in = whole(got, 1), whole(got, 3)
    left_out = quarter(whole(got, 0), mate)
    left_in = own_rows(got, 2, mate)
    outs, ins = [], []
    for t in range(4):
        layer = by_i[4 * mate + t]
        part = slice(16 * t, 16 * t + 16)
        outs.append(dot(left_out[part], masked(right_out, table, layer, True), NN))
        ins.append(dot(left_in[part], masked(right_in, table, layer, False), NT))
    send[...] = jnp.concatenate(outs + ins, axis=0).T.reshape(32, 8, 128).astype(BF)


def backward_kernel(spot, got, grads, by_i, by_j, by_k, send):
    mate = spot[0]
    table = block_table()
    left_out, right_out = whole(got, 0), whole(got, 1)
    left_in = quarter(whole(got, 2), mate)
    right_in = quarter(whole(got, 3), mate)
    grad_out_i = quarter(whole(grads, 0), mate)
    grad_out_j = own_rows(grads, 0, mate)
    grad_in = whole(grads, 1)
    results = [[], [], [], []]
    for t in range(4):
        part = slice(16 * t, 16 * t + 16)
        over_j = masked(right_out, table, by_i[4 * mate + t], True)
        results[0].append(dot(grad_out_i[part], over_j, NT))
        over_i = masked(left_out, table, by_j[4 * mate + t], True)
        results[1].append(dot(grad_out_j[part], over_i, NT))
        both = masked(grad_in, table, by_k[4 * mate + t], True)
        results[2].append(dot(right_in[part], both, NN))
        results[3].append(dot(left_in[part], both, NT))
    stacked = jnp.concatenate(results[0] + results[1] + results[2] + results[3], axis=0)
    send[...] = stacked.T.reshape(32, 8, 256).astype(BF)


def middle_kernel(pair, cotangent, got, gates, gain, w_final, updated, send, grad_gate):
    order = pair_order()
    upstream = dot(cotangent[...], order, ((0,), (0,)))
    total = dot(pair[...], order, ((0,), (0,)))
    for t in range(2):
        triangle = got[:, t].astype(F32).reshape(128, 128)
        scaled, inverse = norm(triangle)
        normed = (scaled * gain[t]).astype(BF)
        gate = gates[128 * t : 128 * t + 128]
        final = dot(w_final[t], normed, ((0,), (0,)))
        total = total + gate * final
        grad_final = (upstream * gate).astype(BF)
        grad_gate[128 * t : 128 * t + 128] = (upstream * final * gate * (1.0 - gate)).astype(BF)
        weighted = dot(w_final[t], grad_final) * gain[t]
        send[:, t] = groups(norm_back(weighted, scaled, inverse)).astype(BF)
    updated[...] = dot(order, total.astype(BF), NT).astype(BF)


def last_kernel(
    cotangent, got, proj, grad_gate, scaled_t, inv, gain, w_out, w_in, w_gate, grad_pair
):
    order = pair_order()
    upstream = dot(cotangent[...], order, ((0,), (0,)))
    grad_normed = dot(w_gate[...], grad_gate[...])
    for half, weights in enumerate((w_out, w_in)):
        p = proj[half]
        parts = []
        for side in range(2):
            grad = got[:, 2 * half + side].astype(F32).reshape(128, 128)
            sig = jax.nn.sigmoid(p[256 * side : 256 * side + 128])
            parts.append(grad * p[256 * side + 128 : 256 * side + 256] * sig * (1.0 - sig))
            parts.append(grad * sig)
        grad_normed = grad_normed + dot(
            weights[...], jnp.concatenate(parts, axis=0).astype(BF)
        )
    back = norm_back(grad_normed * gain[...], scaled_t[...], inv[...])
    grad_pair[...] = dot(order, (upstream + back).astype(BF), NT).astype(BF)


def call(kernel, out, *args, scratch=(), spot=False):
    specs = [pl.BlockSpec(memory_space=pltpu.VMEM)] * len(args)
    if spot:
        specs[0] = pl.BlockSpec(memory_space=pltpu.SMEM)
    multi = isinstance(out, list)
    shapes = [jax.ShapeDtypeStruct(s, d) for s, d in (out if multi else [out])]
    outs = [pl.BlockSpec(memory_space=pltpu.VMEM)] * len(shapes)
    result = pl.pallas_call(
        kernel,
        out_shape=shapes,
        in_specs=specs,
        out_specs=outs,
        scratch_shapes=[pltpu.VMEM(s, F32) for s in scratch],
        compiler_params=pltpu.CompilerParams(vmem_limit_bytes=32 * 1024 * 1024),
    )(*args)
    return result if multi else result[0]


def exchange(values, axis):
    return lax.all_to_all(values, axis, 0, 0, tiled=True)


def to_channels(send):
    amount = send.shape[1]
    got = exchange(send, "row")
    spread = call(
        spread_kernel,
        ((8, 4, amount, 8, 256), BF),
        got,
        scratch=[(8, amount, 8, 256)],
    )
    return exchange(spread.reshape(32, amount, 8, 256), "col")


def to_pairs(send):
    width = send.shape[2]
    amount = width // 64
    got = exchange(send, "col").reshape(8, 4, 8, width)
    back = call(
        collect_kernel,
        ((4, 4, amount, 8, 128), BF),
        got,
        scratch=[(8, 4, 8, width), (4, 4, amount, 8, 128)],
    )
    return exchange(back.reshape(16, amount, 8, 128), "row")


def on_device(
    pair_rep, cotangent, contact, norm_gain, w_out_proj, w_in_proj, update_gain, w_gate, w_final
):
    pair = pair_rep.reshape(128, 128)
    upstream = cotangent.reshape(128, 128)
    gain = norm_gain.reshape(128, 1)
    update = update_gain.reshape(2, 128, 1)
    mate = (lax.axis_index("col") & 3).reshape(1)
    by_i = contact.astype(BF)
    by_j = jnp.transpose(by_i, (1, 0, 2))
    by_k = jnp.transpose(by_i, (2, 0, 1))

    send, proj, gates, scaled_t, inv = call(
        first_kernel,
        [
            ((16, 4, 8, 128), BF),
            ((2, 512, 128), F32),
            ((256, 128), F32),
            ((128, 128), F32),
            ((1, 128), F32),
        ],
        pair,
        gain,
        w_out_proj,
        w_in_proj,
        w_gate,
    )
    sides = to_channels(send)
    triangles = call(forward_kernel, ((32, 8, 128), BF), mate, sides, by_i, spot=True)
    updated, send, grad_gate = call(
        middle_kernel,
        [((128, 128), BF), ((16, 2, 8, 128), BF), ((256, 128), BF)],
        pair,
        upstream,
        to_pairs(triangles),
        gates,
        update,
        w_final,
    )
    grads = call(
        backward_kernel,
        ((32, 8, 256), BF),
        mate,
        sides,
        to_channels(send),
        by_i,
        by_j,
        by_k,
        spot=True,
    )
    grad_pair = call(
        last_kernel,
        ((128, 128), BF),
        upstream,
        to_pairs(grads),
        proj,
        grad_gate,
        scaled_t,
        inv,
        gain,
        w_out_proj,
        w_in_proj,
        w_gate,
    )
    return (updated.reshape(pair_rep.shape), grad_pair.reshape(pair_rep.shape))


def solution(mesh):
    in_specs = (P("row", "col", None), P("row", "col", None), P(), P(), P(), P(), P(), P(), P())
    out_specs = (P("row", "col", None), P("row", "col", None))
    return jax.shard_map(
        on_device, mesh=mesh, in_specs=in_specs, out_specs=out_specs, check_vma=False
    )
```

```python
import functools

import jax
import jax.numpy as jnp
from jax import lax
from jax.experimental import pallas as pl
from jax.experimental.pallas import tpu as pltpu
from jax.sharding import PartitionSpec as P


EPSILON = 1e-05
BF = jnp.bfloat16
F32 = jnp.float32


def dot(a, b, dims=((1,), (0,))):
    return lax.dot_general(a, b, (dims, ((), ())), preferred_element_type=F32)


def norm(values):
    center = jnp.mean(values, axis=0, keepdims=True)
    shifted = values - center
    inverse = lax.rsqrt(jnp.mean(shifted * shifted, axis=0, keepdims=True) + EPSILON)
    return shifted * inverse, inverse


def norm_back(weighted, scaled, inverse):
    first = jnp.mean(weighted, axis=0, keepdims=True)
    second = jnp.mean(weighted * scaled, axis=0, keepdims=True)
    return inverse * (weighted - first - scaled * second)


def pair_order():
    here = lax.broadcasted_iota(jnp.int32, (128, 128), 0)
    there = lax.broadcasted_iota(jnp.int32, (128, 128), 1)
    same = (here >> 3 == (there & 15)) & ((here & 7) == there >> 4)
    return same.astype(F32).astype(BF)


def groups(values):
    return values.reshape(16, 8, 128)


def first_kernel(pair, gain, w_out, w_in, w_gate, send, proj, gates, scaled_t, inv):
    pair_t = dot(pair[...], pair_order(), ((0,), (0,)))
    scaled, inverse = norm(pair_t)
    normed = (scaled * gain[...]).astype(BF)
    scaled_t[...] = scaled
    inv[...] = inverse
    for half, weights in enumerate((w_out, w_in)):
        p = dot(weights[...], normed, ((0,), (0,)))
        proj[half] = p
        send[:, 2 * half] = groups(jax.nn.sigmoid(p[0:128]) * p[128:256]).astype(BF)
        send[:, 2 * half + 1] = groups(jax.nn.sigmoid(p[256:384]) * p[384:512]).astype(BF)
    gates[...] = jax.nn.sigmoid(dot(w_gate[...], normed, ((0,), (0,))))


def swap_groups(rows):
    rows = list(rows)
    group = lax.broadcasted_iota(jnp.int32, rows[0].shape, rows[0].ndim - 1) >> 4
    last = rows[0].ndim - 1
    for step in (4, 2, 1):
        low = (group & step) == 0
        for a in range(8):
            if a & step:
                continue
            x, y = rows[a], rows[a + step]
            rows[a] = jnp.where(low, x, pltpu.roll(y, 16 * step, last))
            rows[a + step] = jnp.where(low, pltpu.roll(x, 128 - 16 * step, last), y)
    return rows


def lower_lanes(shape):
    return lax.broadcasted_iota(jnp.int32, shape, len(shape) - 1) < 64


def spread_kernel(full, parts, got, send, held_full, held_parts):
    amount = got.shape[1]
    low = lower_lanes((8, 128))
    for half in range(2):
        rows = swap_groups(
            [got[8 * half + r].astype(F32).reshape(amount * 8, 128) for r in range(8)]
        )
        for q in range(8):
            pieces = [rows[q][8 * a : 8 * a + 8] for a in range(amount)]
            held_full[:, q, 128 * half : 128 * half + 128] = pieces[full]
            for n, pair in enumerate(parts):
                first, second = pieces[pair[0]], pieces[pair[-1]]
                lanes = slice(128 * n, 128 * n + 128)
                held_parts[:, 2 * half, q, lanes] = jnp.where(
                    low, first, pltpu.roll(second, 64, 1)
                )
                held_parts[:, 2 * half + 1, q, lanes] = jnp.where(
                    low, pltpu.roll(first, 64, 1), second
                )
    values = held_full[...].astype(BF)
    for mate in range(4):
        send[:, mate, :, 0:256] = values
    send[:, :, :, 256:] = held_parts[...].astype(BF)


def collect_kernel(full, parts, got, send, held, out):
    held[...] = got[...].astype(F32)
    low = lower_lanes((8, 128))
    for half in range(2):
        rows = []
        for q in range(8):
            lanes = slice(128 * half, 128 * half + 128)
            total = held[:, 0, q, lanes]
            for mate in range(1, 4):
                total = total + held[:, mate, q, lanes]
            rows.append(total)
        for g, values in enumerate(swap_groups(rows)):
            out[8 * half + g, full] = values
        for n, pair in enumerate(parts):
            lanes = slice(256 + 128 * n, 384 + 128 * n)
            for place, array in enumerate(pair):
                rows = []
                for q in range(8):
                    x = held[:, 2 * half, q, lanes]
                    y = held[:, 2 * half + 1, q, lanes]
                    if place == 0:
                        rows.append(jnp.where(low, x, pltpu.roll(y, 64, 1)))
                    else:
                        rows.append(jnp.where(low, pltpu.roll(x, 64, 1), y))
                for g, values in enumerate(swap_groups(rows)):
                    out[8 * half + g, array] = values
    send[...] = out[...].astype(BF)


def whole(got):
    return got[:, :, 0:256].astype(F32).reshape(256, 256)


def quarters(got, n):
    return got[:, :, 256 + 128 * n : 384 + 128 * n].astype(F32).reshape(256, 128).T.astype(BF)


def block_table():
    place = lax.broadcasted_iota(jnp.int32, (256, 16), 0) >> 4
    label = lax.broadcasted_iota(jnp.int32, (256, 16), 1)
    return (place == label).astype(F32).astype(BF)


def spread_mask(table, layer):
    side = dot(table, layer, NT).astype(BF)
    return dot(side, table, NT)


NN = ((1,), (0,))
NT = ((1,), (1,))
TN = ((0,), (0,))


def forward_kernel(spot, got, by_i, by_k, send):
    mate = spot[0]
    table = block_table()
    right_out = whole(got).astype(BF)
    mixed = quarters(got, 0)
    left_out, left_in = mixed[0:64], mixed[64:128]
    right_in = quarters(got, 1)[0:64]
    outs, ins = [], None
    for t in range(4):
        part = slice(16 * t, 16 * t + 16)
        mask = spread_mask(table, by_i[4 * mate + t]).astype(BF)
        outs.append(dot(left_out[part], right_out * mask, NN))
        mask = spread_mask(table, by_k[4 * mate + t])
        term = dot(right_in[part], left_in[part], TN) * mask
        ins = term if ins is None else ins + term
    outs = jnp.concatenate(outs + [jnp.zeros((64, 256), F32)], axis=0).T
    send[:, :, 0:256] = ins.reshape(32, 8, 256).astype(BF)
    send[:, :, 256:384] = outs.reshape(32, 8, 128).astype(BF)


def backward_kernel(spot, got, grads, by_i, by_k, send):
    mate = spot[0]
    table = block_table()
    right_out = whole(got).astype(BF)
    mixed = quarters(got, 0)
    left_out, left_in = mixed[0:64], mixed[64:128]
    right_in = quarters(got, 1)[0:64]
    grad_in = whole(grads).astype(BF)
    grad_out = quarters(grads, 0)[0:64]
    grad_left_out, grad_left_in, grad_right_in, grad_right_out = [], [], [], None
    for t in range(4):
        part = slice(16 * t, 16 * t + 16)
        mask = spread_mask(table, by_i[4 * mate + t])
        grad_left_out.append(dot(grad_out[part], right_out * mask.astype(BF), NT))
        term = dot(left_out[part], grad_out[part], TN) * mask
        grad_right_out = term if grad_right_out is None else grad_right_out + term
        both = grad_in * spread_mask(table, by_k[4 * mate + t]).astype(BF)
        grad_left_in.append(dot(right_in[part], both, NN))
        grad_right_in.append(dot(left_in[part], both, NT))
    rest = grad_left_out + grad_left_in + grad_right_in + [jnp.zeros((64, 256), F32)]
    send[:, :, 0:256] = grad_right_out.reshape(32, 8, 256).astype(BF)
    send[:, :, 256:512] = jnp.concatenate(rest, axis=0).T.reshape(32, 8, 256).astype(BF)


def middle_kernel(pair, cotangent, got, gates, gain, w_final, updated, send, grad_gate):
    order = pair_order()
    upstream = dot(cotangent[...], order, ((0,), (0,)))
    total = dot(pair[...], order, ((0,), (0,)))
    for t in range(2):
        triangle = got[:, t].astype(F32).reshape(128, 128)
        scaled, inverse = norm(triangle)
        normed = (scaled * gain[t]).astype(BF)
        gate = gates[128 * t : 128 * t + 128]
        final = dot(w_final[t], normed, ((0,), (0,)))
        total = total + gate * final
        grad_final = (upstream * gate).astype(BF)
        grad_gate[128 * t : 128 * t + 128] = (upstream * final * gate * (1.0 - gate)).astype(BF)
        weighted = dot(w_final[t], grad_final) * gain[t]
        send[:, t] = groups(norm_back(weighted, scaled, inverse)).astype(BF)
    updated[...] = dot(order, total.astype(BF), NT).astype(BF)


def last_kernel(
    cotangent, got, proj, grad_gate, scaled_t, inv, gain, w_out, w_in, w_gate, grad_pair
):
    order = pair_order()
    upstream = dot(cotangent[...], order, ((0,), (0,)))
    grad_normed = dot(w_gate[...], grad_gate[...])
    for half, weights in enumerate((w_out, w_in)):
        p = proj[half]
        parts = []
        for side in range(2):
            grad = got[:, 2 * half + side].astype(F32).reshape(128, 128)
            sig = jax.nn.sigmoid(p[256 * side : 256 * side + 128])
            parts.append(grad * p[256 * side + 128 : 256 * side + 256] * sig * (1.0 - sig))
            parts.append(grad * sig)
        grad_normed = grad_normed + dot(
            weights[...], jnp.concatenate(parts, axis=0).astype(BF)
        )
    back = norm_back(grad_normed * gain[...], scaled_t[...], inv[...])
    grad_pair[...] = dot(order, (upstream + back).astype(BF), NT).astype(BF)


def call(kernel, out, *args, scratch=(), spot=False):
    specs = [pl.BlockSpec(memory_space=pltpu.VMEM)] * len(args)
    if spot:
        specs[0] = pl.BlockSpec(memory_space=pltpu.SMEM)
    multi = isinstance(out, list)
    shapes = [jax.ShapeDtypeStruct(s, d) for s, d in (out if multi else [out])]
    outs = [pl.BlockSpec(memory_space=pltpu.VMEM)] * len(shapes)
    result = pl.pallas_call(
        kernel,
        out_shape=shapes,
        in_specs=specs,
        out_specs=outs,
        scratch_shapes=[pltpu.VMEM(s, F32) for s in scratch],
        compiler_params=pltpu.CompilerParams(vmem_limit_bytes=32 * 1024 * 1024),
    )(*args)
    return result if multi else result[0]


def exchange(values, axis):
    return lax.all_to_all(values, axis, 0, 0, tiled=True)


def to_channels(send, full, parts):
    got = exchange(send, "row")
    width = 256 + 128 * len(parts)
    spread = call(
        functools.partial(spread_kernel, full, parts),
        ((8, 4, 8, width), BF),
        got,
        scratch=[(8, 8, 256), (8, 4, 8, width - 256)],
    )
    return exchange(spread.reshape(32, 8, width), "col")


def to_pairs(send, full, parts):
    width = send.shape[2]
    amount = 1 + sum(len(pair) for pair in parts)
    got = exchange(send, "col").reshape(8, 4, 8, width)
    back = call(
        functools.partial(collect_kernel, full, parts),
        ((16, amount, 8, 128), BF),
        got,
        scratch=[(8, 4, 8, width), (16, amount, 8, 128)],
    )
    return exchange(back, "row")


def on_device(
    pair_rep, cotangent, contact, norm_gain, w_out_proj, w_in_proj, update_gain, w_gate, w_final
):
    pair = pair_rep.reshape(128, 128)
    upstream = cotangent.reshape(128, 128)
    gain = norm_gain.reshape(128, 1)
    update = update_gain.reshape(2, 128, 1)
    mate = (lax.axis_index("col") & 3).reshape(1)
    by_i = contact.astype(BF)
    by_k = jnp.transpose(by_i, (2, 0, 1))

    send, proj, gates, scaled_t, inv = call(
        first_kernel,
        [
            ((16, 4, 8, 128), BF),
            ((2, 512, 128), F32),
            ((256, 128), F32),
            ((128, 128), F32),
            ((1, 128), F32),
        ],
        pair,
        gain,
        w_out_proj,
        w_in_proj,
        w_gate,
    )
    sides = to_channels(send, 1, ((0, 2), (3,)))
    triangles = call(forward_kernel, ((32, 8, 384), BF), mate, sides, by_i, by_k, spot=True)
    updated, send, grad_gate = call(
        middle_kernel,
        [((128, 128), BF), ((16, 2, 8, 128), BF), ((256, 128), BF)],
        pair,
        upstream,
        to_pairs(triangles, 1, ((0,),)),
        gates,
        update,
        w_final,
    )
    grads = call(
        backward_kernel,
        ((32, 8, 512), BF),
        mate,
        sides,
        to_channels(send, 1, ((0,),)),
        by_i,
        by_k,
        spot=True,
    )
    grad_pair = call(
        last_kernel,
        ((128, 128), BF),
        upstream,
        to_pairs(grads, 1, ((0, 2), (3,))),
        proj,
        grad_gate,
        scaled_t,
        inv,
        gain,
        w_out_proj,
        w_in_proj,
        w_gate,
    )
    return (updated.reshape(pair_rep.shape), grad_pair.reshape(pair_rep.shape))


def solution(mesh):
    in_specs = (P("row", "col", None), P("row", "col", None), P(), P(), P(), P(), P(), P(), P())
    out_specs = (P("row", "col", None), P("row", "col", None))
    return jax.shard_map(
        on_device, mesh=mesh, in_specs=in_specs, out_specs=out_specs, check_vma=False
    )
```

```python
import functools

import jax
import jax.numpy as jnp
from jax import lax
from jax.experimental import pallas as pl
from jax.experimental.pallas import tpu as pltpu
from jax.sharding import Mesh
from jax.sharding import PartitionSpec as P


PLANE = ("x", "y", "core")
DEPTH = ("zl", "zh")
EPSILON = 1e-05
BF = jnp.bfloat16
F32 = jnp.float32


def dot(a, b, dims=((1,), (0,))):
    return lax.dot_general(a, b, (dims, ((), ())), preferred_element_type=F32)


def norm(values):
    center = jnp.mean(values, axis=0, keepdims=True)
    shifted = values - center
    inverse = lax.rsqrt(jnp.mean(shifted * shifted, axis=0, keepdims=True) + EPSILON)
    return shifted * inverse, inverse


def norm_back(weighted, scaled, inverse):
    first = jnp.mean(weighted, axis=0, keepdims=True)
    second = jnp.mean(weighted * scaled, axis=0, keepdims=True)
    return inverse * (weighted - first - scaled * second)


def pair_order():
    here = lax.broadcasted_iota(jnp.int32, (128, 128), 0)
    there = lax.broadcasted_iota(jnp.int32, (128, 128), 1)
    same = (here >> 3 == (there & 15)) & ((here & 7) == there >> 4)
    return same.astype(F32).astype(BF)


def column(gain):
    return jnp.broadcast_to(gain, (128, 128)).T


def put(held, array, values):
    for n in range(4):
        held[:, 4 * array + n] = values[32 * n : 32 * n + 32]


def take(got, array):
    return jnp.concatenate([got[:, 4 * array + n] for n in range(4)], axis=0)


def fetch(pairs, arrived):
    copies = [
        pltpu.make_async_copy(there, here, arrived.at[n]) for n, (there, here) in enumerate(pairs)
    ]
    for copy in copies:
        copy.start()
    return copies


def first_kernel(*refs):
    far, (send, proj, gates, scaled_t, inv), near = refs[:5], refs[5:10], refs[10:15]
    held, arrived = refs[15:]
    copies = fetch(list(zip(far, near)), arrived)
    pair, gain, w_out, w_in, w_gate = near
    copies[0].wait()
    pair_t = dot(pair[...], pair_order(), ((0,), (0,)))
    scaled, inverse = norm(pair_t)
    copies[1].wait()
    normed = (scaled * column(gain[...])).astype(BF)
    scaled_t[...] = scaled
    inv[...] = inverse
    for half, weights in enumerate((w_out, w_in)):
        copies[2 + half].wait()
        p = dot(weights[...], normed, ((0,), (0,)))
        proj[half] = p
        put(held, 2 * half, jax.nn.sigmoid(p[0:128]) * p[128:256])
        put(held, 2 * half + 1, jax.nn.sigmoid(p[256:384]) * p[384:512])
    send[...] = held[...].astype(BF)
    copies[4].wait()
    gates[...] = jax.nn.sigmoid(dot(w_gate[...], normed, ((0,), (0,))))


def swap_groups(rows):
    rows = list(rows)
    group = lax.broadcasted_iota(jnp.int32, rows[0].shape, 1) >> 4
    step = len(rows) // 2
    while step:
        low = (group & step) == 0
        for a in range(len(rows)):
            if a & step:
                continue
            x, y = rows[a], rows[a + step]
            rows[a] = jnp.where(low, x, pltpu.roll(y, 16 * step, 1))
            rows[a + step] = jnp.where(low, pltpu.roll(x, 128 - 16 * step, 1), y)
        step //= 2
    return rows


def spread_kernel(full, parts, got, send, held_full, held_parts):
    by_y = []
    for y in range(4):
        rows = swap_groups(
            [got[8 * x + 2 * y + core].astype(F32) for core in range(2) for x in range(4)]
        )
        for q in range(8):
            held_full[:, 8 * y + q] = rows[q][4 * full : 4 * full + 4]
        by_y.append(rows)
    for q in range(8):
        for mate, rows in enumerate(swap_groups([by_y[y][q] for y in range(4)])):
            for n, a in enumerate(parts):
                held_parts[:, mate, 8 * n + q] = rows[4 * a : 4 * a + 4]
    values = held_full[...].astype(BF)
    for mate in range(4):
        send[:, mate, 0:32] = values
    send[:, :, 32:] = held_parts[...].astype(BF)


def collect_kernel(full, parts, got, send, held, held_parts, out):
    values = got[...].astype(F32)
    held[...] = values[:, 0, 0:32] + values[:, 1, 0:32] + values[:, 2, 0:32] + values[:, 3, 0:32]
    held_parts[...] = values[:, :, 32:]
    for a in (full, *parts):
        by_q = []
        for q in range(8):
            if a == full:
                by_q.append([held[:, 8 * y + q] for y in range(4)])
            else:
                row = 8 * parts.index(a) + q
                by_q.append(swap_groups([held_parts[:, mate, row] for mate in range(4)]))
        for y in range(4):
            for g, rows in enumerate(swap_groups([by_q[q][y] for q in range(8)])):
                out[8 * (g & 3) + 2 * y + (g >> 2), 4 * a : 4 * a + 4] = rows
    send[...] = out[...].astype(BF)


def swap_halves(first, second):
    low = lax.broadcasted_iota(jnp.int32, first.shape, 1) < 64
    return (
        jnp.where(low, first, pltpu.roll(second, 64, 1)),
        jnp.where(low, pltpu.roll(first, 64, 1), second),
    )


def reorder():
    residue = lax.broadcasted_iota(jnp.int32, (256, 256), 0)
    place = lax.broadcasted_iota(jnp.int32, (256, 256), 1)
    return one_hot(residue, q_block(place) * 16 + (place >> 7) * 8 + (place & 7))


def whole(got):
    tiles = [got[zl, :, 0:32].astype(F32).reshape(128, 128) for zl in range(4)]
    left = swap_halves(tiles[0], tiles[1])
    right = swap_halves(tiles[2], tiles[3])
    values = jnp.concatenate(
        [jnp.concatenate([left[core], right[core]], axis=1) for core in range(2)], axis=0
    )
    return dot(values.astype(BF), reorder()).astype(BF)


def quarter(got, n):
    by_zh = []
    for zh in range(4):
        tiles = [got[zl, zh, 32 + 8 * n : 40 + 8 * n].astype(F32) for zl in range(4)]
        by_zh += swap_groups(tiles)
    turned = jnp.concatenate(by_zh, axis=0).T
    return jnp.concatenate([turned[0:64], turned[64:128]], axis=1).astype(BF)


def send_whole(send, values):
    values = dot(values.astype(BF), reorder(), NT)
    for half in range(2):
        lanes = slice(128 * half, 128 * half + 128)
        tiles = swap_halves(values[0:128, lanes], values[128:256, lanes])
        for n in range(2):
            send[2 * half + n, :, 0:32] = tiles[n].reshape(4, 32, 128).astype(BF)


def send_quarter(send, n, held, values):
    turned = jnp.concatenate([values[:, 0:128], values[:, 128:256]], axis=0).T
    for zh in range(4):
        rows = [turned[32 * zh + 8 * y : 32 * zh + 8 * y + 8] for y in range(4)]
        for zl, tile in enumerate(swap_groups(rows)):
            held[zl, zh, 8 * n : 8 * n + 8] = tile


NN = ((1,), (0,))
NT = ((1,), (1,))
TN = ((0,), (0,))


def one_hot(label, values):
    return (label == values).astype(F32).astype(BF)


def q_block(place):
    return ((place >> 3) & 3) * 4 + ((place >> 5) & 3)


def mask_tables():
    place = lax.broadcasted_iota(jnp.int32, (256, 16), 0)
    label = lax.broadcasted_iota(jnp.int32, (256, 16), 1)
    q_table = one_hot(label, q_block(place))
    place = lax.broadcasted_iota(jnp.int32, (256, 256), 0)
    label = lax.broadcasted_iota(jnp.int32, (256, 256), 1)
    j_table, i_table = one_hot(label & 15, q_block(place)), one_hot(label >> 4, q_block(place))
    return q_table, j_table, i_table


def mask_out(tables, contact, i):
    side = dot(tables[0], contact[i].astype(F32).astype(BF), NT).astype(BF)
    return dot(side, tables[0], NT)


def mask_in(tables, by_k, k):
    return dot(tables[1] * by_k[pl.ds(k, 1)].astype(BF), tables[2], NT)


def forward_kernel(spot, got, contact, flat, send, by_k, held):
    mate = spot[0]
    tables = mask_tables()
    by_k[...] = flat[...].astype(F32).T
    right_out = whole(got)
    left_out, left_in, right_in = [quarter(got, n) for n in range(3)]
    outs, ins = [], None
    for t in range(4):
        part = slice(16 * t, 16 * t + 16)
        mask = mask_out(tables, contact, 4 * t + mate).astype(BF)
        outs.append(dot(left_out[part], right_out * mask, NN))
        mask = mask_in(tables, by_k, 4 * t + mate)
        term = dot(right_in[part], left_in[part], TN) * mask
        ins = term if ins is None else ins + term
    send_whole(send, ins)
    send_quarter(send, 0, held, jnp.concatenate(outs, axis=0))
    send[:, :, 32:] = held[...].astype(BF)


def backward_kernel(spot, got, grads, contact, flat, send, by_k, held):
    mate = spot[0]
    tables = mask_tables()
    by_k[...] = flat[...].astype(F32).T
    right_out = whole(got)
    left_out, left_in, right_in = [quarter(got, n) for n in range(3)]
    grad_in = whole(grads)
    grad_out = quarter(grads, 0)
    grad_left_out, grad_left_in, grad_right_in, grad_right_out = [], [], [], None
    for t in range(4):
        part = slice(16 * t, 16 * t + 16)
        mask = mask_out(tables, contact, 4 * t + mate)
        grad_left_out.append(dot(grad_out[part], right_out * mask.astype(BF), NT))
        term = dot(left_out[part], grad_out[part], TN) * mask
        grad_right_out = term if grad_right_out is None else grad_right_out + term
        both = grad_in * mask_in(tables, by_k, 4 * t + mate).astype(BF)
        grad_left_in.append(dot(right_in[part], both, NN))
        grad_right_in.append(dot(left_in[part], both, NT))
    send_whole(send, grad_right_out)
    for n, values in enumerate((grad_left_out, grad_left_in, grad_right_in)):
        send_quarter(send, n, held, jnp.concatenate(values, axis=0))
    send[:, :, 32:] = held[...].astype(BF)


def middle_kernel(pair, cotangent, got, gates, gain, w_final, updated, send, grad_gate, held):
    order = pair_order()
    upstream = dot(cotangent[...], order, TN)
    total = dot(pair[...], order, TN)
    arrived = got[...].astype(F32)
    for t in range(2):
        scaled, inverse = norm(take(arrived, t))
        gain_t = column(gain[t : t + 1])
        normed = (scaled * gain_t).astype(BF)
        gate = gates[128 * t : 128 * t + 128]
        final = dot(w_final[t], normed, TN)
        total = total + gate * final
        grad_final = (upstream * gate).astype(BF)
        grad_gate[128 * t : 128 * t + 128] = (upstream * final * gate * (1.0 - gate)).astype(BF)
        weighted = dot(w_final[t], grad_final) * gain_t
        put(held, t, norm_back(weighted, scaled, inverse))
    send[...] = held[...].astype(BF)
    updated[...] = dot(order, total.astype(BF), NT).astype(BF)


def last_kernel(
    cotangent, got, proj, grad_gate, scaled_t, inv, gain, w_out, w_in, w_gate, grad_pair
):
    order = pair_order()
    upstream = dot(cotangent[...], order, TN)
    arrived = got[...].astype(F32)
    grad_normed = dot(w_gate[...], grad_gate[...])
    for half, weights in enumerate((w_out, w_in)):
        p = proj[half]
        parts = []
        for side in range(2):
            grad = take(arrived, 2 * half + side)
            sig = jax.nn.sigmoid(p[256 * side : 256 * side + 128])
            parts.append(grad * p[256 * side + 128 : 256 * side + 256] * sig * (1.0 - sig))
            parts.append(grad * sig)
        grad_normed = grad_normed + dot(
            weights[...], jnp.concatenate(parts, axis=0).astype(BF)
        )
    back = norm_back(grad_normed * column(gain[...]), scaled_t[...], inv[...])
    grad_pair[...] = dot(order, (upstream + back).astype(BF), NT).astype(BF)


def call(kernel, out, *args, scratch=(), spot=False, far=False):
    place = pl.ANY if far else pltpu.VMEM
    specs = [pl.BlockSpec(memory_space=place)] * len(args)
    if spot:
        specs[0] = pl.BlockSpec(memory_space=pltpu.SMEM)
    multi = isinstance(out, list)
    shapes = [jax.ShapeDtypeStruct(s, d) for s, d in (out if multi else [out])]
    outs = [pl.BlockSpec(memory_space=pltpu.VMEM)] * len(shapes)
    buffers = [pltpu.VMEM(s, F32) for s in scratch]
    params = pltpu.CompilerParams(vmem_limit_bytes=32 * 1024 * 1024)
    if far:
        buffers = [pltpu.VMEM(x.shape, x.dtype) for x in args] + buffers
        buffers.append(pltpu.SemaphoreType.DMA((len(args),)))
        params = None
    result = pl.pallas_call(
        kernel,
        out_shape=shapes,
        in_specs=specs,
        out_specs=outs,
        scratch_shapes=buffers,
        compiler_params=params,
    )(*args)
    return result if multi else result[0]


def exchange(values, axis):
    return lax.all_to_all(values, axis, 0, 0, tiled=True)


def to_channels(send, full, parts):
    rows = 32 + 8 * len(parts)
    spread = call(
        functools.partial(spread_kernel, full, parts),
        ((4, 4, rows, 128), BF),
        exchange(send, PLANE),
        scratch=[(4, 32, 128), (4, 4, rows - 32, 128)],
    )
    return exchange(spread.reshape(16, rows, 128), DEPTH).reshape(4, 4, rows, 128)


def to_pairs(send, full, parts):
    rows = 32 + 8 * len(parts)
    amount = 1 + len(parts)
    back = call(
        functools.partial(collect_kernel, full, parts),
        ((32, 4 * amount, 128), BF),
        exchange(send.reshape(16, rows, 128), DEPTH).reshape(4, 4, rows, 128),
        scratch=[(4, 32, 128), (4, 4, rows - 32, 128), (32, 4 * amount, 128)],
    )
    return exchange(back, PLANE)


def my_mate():
    return lax.axis_index("zh")


def on_device(
    pair_rep, cotangent, contact, norm_gain, w_out_proj, w_in_proj, update_gain, w_gate, w_final
):
    pair = pair_rep.reshape(128, 128)
    upstream = cotangent.reshape(128, 128)
    gain = norm_gain.reshape(1, 128)
    mate = my_mate().reshape(1)
    flat = contact.reshape(256, 16)

    send, proj, gates, scaled_t, inv = call(
        first_kernel,
        [
            ((32, 16, 128), BF),
            ((2, 512, 128), F32),
            ((256, 128), F32),
            ((128, 128), F32),
            ((1, 128), F32),
        ],
        pair,
        gain,
        w_out_proj,
        w_in_proj,
        w_gate,
        scratch=[(32, 16, 128)],
        far=True,
    )
    sides = to_channels(send, 1, (0, 2, 3))
    triangles = call(
        forward_kernel,
        ((4, 4, 40, 128), BF),
        mate,
        sides,
        contact,
        flat,
        scratch=[(16, 256), (4, 4, 8, 128)],
        spot=True,
    )
    updated, send, grad_gate = call(
        middle_kernel,
        [((128, 128), BF), ((32, 8, 128), BF), ((256, 128), BF)],
        pair,
        upstream,
        to_pairs(triangles, 1, (0,)),
        gates,
        update_gain,
        w_final,
        scratch=[(32, 8, 128)],
    )
    grads = call(
        backward_kernel,
        ((4, 4, 56, 128), BF),
        mate,
        sides,
        to_channels(send, 1, (0,)),
        contact,
        flat,
        scratch=[(16, 256), (4, 4, 24, 128)],
        spot=True,
    )
    grad_pair = call(
        last_kernel,
        ((128, 128), BF),
        upstream,
        to_pairs(grads, 1, (0, 2, 3)),
        proj,
        grad_gate,
        scaled_t,
        inv,
        gain,
        w_out_proj,
        w_in_proj,
        w_gate,
    )
    return (updated.reshape(pair_rep.shape), grad_pair.reshape(pair_rep.shape))


def solution(mesh):
    fine = Mesh(mesh.devices.reshape(4, 4, 4, 4, 2), ("zl", "x", "y", "zh", "core"))
    block = P(("zl", "x"), ("y", "zh", "core"), None)
    in_specs = (block, block, P(), P(), P(), P(), P(), P(), P())
    return jax.shard_map(
        on_device, mesh=fine, in_specs=in_specs, out_specs=(block, block), check_vma=False
    )
```

```python
import functools

import jax
import jax.numpy as jnp
from jax import lax
from jax.experimental import pallas as pl
from jax.experimental.pallas import tpu as pltpu
from jax.sharding import Mesh
from jax.sharding import PartitionSpec as P


PLANE = ("x", "y", "core")
DEPTH = ("zl", "zh")
EPSILON = 1e-05
BF = jnp.bfloat16
F32 = jnp.float32


def dot(a, b, dims=((1,), (0,))):
    return lax.dot_general(a, b, (dims, ((), ())), preferred_element_type=F32)


def norm(values):
    center = jnp.mean(values, axis=0, keepdims=True)
    shifted = values - center
    inverse = lax.rsqrt(jnp.mean(shifted * shifted, axis=0, keepdims=True) + EPSILON)
    return shifted * inverse, inverse


def norm_back(weighted, scaled, inverse):
    first = jnp.mean(weighted, axis=0, keepdims=True)
    second = jnp.mean(weighted * scaled, axis=0, keepdims=True)
    return inverse * (weighted - first - scaled * second)


def pair_order():
    here = lax.broadcasted_iota(jnp.int32, (128, 128), 0)
    there = lax.broadcasted_iota(jnp.int32, (128, 128), 1)
    same = (here >> 3 == (there & 15)) & ((here & 7) == there >> 4)
    return same.astype(F32).astype(BF)


def column(gain):
    return jnp.broadcast_to(gain, (128, 128)).T


def groups(values):
    return values.reshape(16, 8, 128).astype(BF)


def take(got, array):
    return got[:, 8 * array : 8 * array + 8].astype(F32).reshape(128, 128)


def fetch(pairs, arrived):
    copies = [
        pltpu.make_async_copy(there, here, arrived.at[n]) for n, (there, here) in enumerate(pairs)
    ]
    for copy in copies:
        copy.start()
    return copies


def first_kernel(*refs):
    far, (send, proj, gates, scaled_t), near = refs[:6], refs[6:10], refs[10:16]
    copies = fetch(list(zip(far, near)), refs[16])
    pair, gain, w_out, w_in, w_gate, update = near
    copies[0].wait()
    pair_t = dot(pair[...], pair_order(), ((0,), (0,)))
    scaled, inverse = norm(pair_t)
    copies[1].wait()
    normed = (scaled * column(gain[...])).astype(BF)
    scaled_t[0:128] = scaled
    scaled_t[128:129] = inverse
    scaled_t[129:130] = gain[...]
    for half, weights in enumerate((w_out, w_in)):
        copies[2 + half].wait()
        p = dot(weights[...], normed, ((0,), (0,)))
        proj[half] = p
        for side in range(2):
            part = 256 * side
            gated = jax.nn.sigmoid(p[part : part + 128]) * p[part + 128 : part + 256]
            row = 16 * half + 8 * side
            send[:, row : row + 8] = groups(gated)
    copies[4].wait()
    copies[5].wait()
    gates[0:256] = jax.nn.sigmoid(dot(w_gate[...], normed, ((0,), (0,))))
    gates[256:258] = update[...]


def swap_groups(rows):
    rows = list(rows)
    group = lax.broadcasted_iota(jnp.int32, rows[0].shape, 1) >> 4
    step = len(rows) // 2
    while step:
        low = (group & step) == 0
        for a in range(len(rows)):
            if a & step:
                continue
            x, y = rows[a], rows[a + step]
            rows[a] = jnp.where(low, x, pltpu.roll(y, 16 * step, 1))
            rows[a + step] = jnp.where(low, pltpu.roll(x, 128 - 16 * step, 1), y)
        step //= 2
    return rows


def spread_kernel(full, parts, got, send, held_full, held_parts):
    for high in range(2):
        rows = swap_groups(
            [got[4 * zl + 2 * high + low].astype(F32) for low in range(2) for zl in range(4)]
        )
        for q in range(8):
            held_full[:, 8 * high + q] = rows[q][8 * full : 8 * full + 8]
            pieces = swap_groups([rows[q][8 * a : 8 * a + 8] for a in parts])
            for mate in range(4):
                held_parts[:, mate, 8 * high + q] = pieces[mate]
    values = held_full[...].astype(BF)
    for mate in range(4):
        send[:, mate, 0:16] = values
    send[:, :, 16:32] = held_parts[...].astype(BF)


def collect_kernel(full, parts, got, send, held, held_parts, out):
    values = got[...].astype(F32)
    held[...] = values[:, 0, 0:16] + values[:, 1, 0:16] + values[:, 2, 0:16] + values[:, 3, 0:16]
    held_parts[...] = values[:, :, 16:32]
    for high in range(2):
        by_q = []
        for q in range(8):
            row = 8 * high + q
            pieces = swap_groups([held_parts[:, mate, row] for mate in range(4)])
            by_q.append({full: held[:, row], **dict(zip(parts, pieces))})
        for a in (full, *parts):
            for g, rows in enumerate(swap_groups([by_q[q][a] for q in range(8)])):
                zh = 2 * high + (g >> 2)
                out[4 * (g & 3) + zh, 8 * a : 8 * a + 8] = rows
    send[...] = out[...].astype(BF)


def swap_halves(first, second):
    low = lax.broadcasted_iota(jnp.int32, first.shape, 1) < 64
    return (
        jnp.where(low, first, pltpu.roll(second, 64, 1)),
        jnp.where(low, pltpu.roll(first, 64, 1), second),
    )


def reorder():
    p = lax.broadcasted_iota(jnp.int32, (256, 256), 0)
    q = lax.broadcasted_iota(jnp.int32, (256, 256), 1)
    residue = ((p >> 4) & 3) * 64 + (p >> 6) * 16 + (p & 15)
    return one_hot(residue, q_block(q) * 16 + ((q >> 4) & 1) * 8 + (q & 7))


def whole(got):
    tiles = [got[x, :, 0:16].astype(F32).reshape(128, 128) for x in range(4)]
    left = swap_halves(tiles[0], tiles[1])
    right = swap_halves(tiles[2], tiles[3])
    values = jnp.concatenate(
        [jnp.concatenate([left[low], right[low]], axis=1) for low in range(2)], axis=0
    )
    return dot(values.astype(BF), reorder()).astype(BF)


def quarters(got, amount):
    tiles = [got[x, :, 16:32].astype(F32).reshape(128, 128) for x in range(4)]
    turned = [values.T for values in swap_groups(tiles)[:amount]]
    return [jnp.concatenate([t[0:64], t[64:128]], axis=1).astype(BF) for t in turned]


def send_whole(send, values):
    values = dot(values.astype(BF), reorder(), NT)
    for half in range(2):
        lanes = slice(128 * half, 128 * half + 128)
        tiles = swap_halves(values[0:128, lanes], values[128:256, lanes])
        for n in range(2):
            send[2 * half + n, :, 0:16] = tiles[n].reshape(8, 16, 128).astype(BF)


def send_quarters(send, arrays):
    rows = []
    for pieces in arrays:
        values = jnp.concatenate(pieces, axis=0)
        rows.append(jnp.concatenate([values[:, 0:128], values[:, 128:256]], axis=0).T)
    while len(rows) < 4:
        rows.append(jnp.zeros((128, 128), F32))
    for x, tile in enumerate(swap_groups(rows)):
        send[x, :, 16:32] = tile.reshape(8, 16, 128).astype(BF)


NN = ((1,), (0,))
NT = ((1,), (1,))
TN = ((0,), (0,))


def one_hot(label, values):
    return (label == values).astype(F32).astype(BF)


def q_block(place):
    return ((place >> 5) & 3) * 4 + ((place >> 3) & 1) * 2 + (place >> 7)


def mask_tables():
    place = lax.broadcasted_iota(jnp.int32, (256, 16), 0)
    label = lax.broadcasted_iota(jnp.int32, (256, 16), 1)
    q_table = one_hot(label, q_block(place))
    place = lax.broadcasted_iota(jnp.int32, (256, 256), 0)
    label = lax.broadcasted_iota(jnp.int32, (256, 256), 1)
    j_table, i_table = one_hot(label & 15, q_block(place)), one_hot(label >> 4, q_block(place))
    return q_table, j_table, i_table


def mask_out(tables, contact, i):
    side = dot(tables[0], contact[i].astype(F32).astype(BF), NT).astype(BF)
    return dot(side, tables[0], NT)


def mask_in(tables, by_k, k):
    return dot(tables[1] * by_k[pl.ds(k, 1)].astype(BF), tables[2], NT)


def forward_kernel(spot, got, contact, flat, send, near, by_k, arrived):
    copies = fetch([(contact, near)], arrived)
    mate = spot[0]
    tables = mask_tables()
    by_k[...] = flat[...].astype(F32).T
    right_out = whole(got)
    left_out, left_in, right_in = quarters(got, 3)
    copies[0].wait()
    outs, ins = [], None
    for t in range(4):
        part = slice(16 * t, 16 * t + 16)
        mask = mask_out(tables, near, 4 * mate + t).astype(BF)
        outs.append(dot(left_out[part], right_out * mask, NN))
        mask = mask_in(tables, by_k, 4 * mate + t)
        term = dot(right_in[part], left_in[part], TN) * mask
        ins = term if ins is None else ins + term
    send_whole(send, ins)
    send_quarters(send, [outs])


def backward_kernel(spot, got, grads, contact, flat, send, near, by_k, arrived):
    copies = fetch([(contact, near)], arrived)
    mate = spot[0]
    tables = mask_tables()
    by_k[...] = flat[...].astype(F32).T
    right_out = whole(got)
    left_out, left_in, right_in = quarters(got, 3)
    grad_in = whole(grads)
    grad_out = quarters(grads, 1)[0]
    copies[0].wait()
    grad_left_out, grad_left_in, grad_right_in, grad_right_out = [], [], [], None
    for t in range(4):
        part = slice(16 * t, 16 * t + 16)
        mask = mask_out(tables, near, 4 * mate + t)
        grad_left_out.append(dot(grad_out[part], right_out * mask.astype(BF), NT))
        term = dot(left_out[part], grad_out[part], TN) * mask
        grad_right_out = term if grad_right_out is None else grad_right_out + term
        both = grad_in * mask_in(tables, by_k, 4 * mate + t).astype(BF)
        grad_left_in.append(dot(right_in[part], both, NN))
        grad_right_in.append(dot(left_in[part], both, NT))
    send_whole(send, grad_right_out)
    send_quarters(send, [grad_left_out, grad_left_in, grad_right_in])


def middle_kernel(pair, cotangent, got, gates, w_final, updated, send, grad_gate):
    order = pair_order()
    upstream = dot(cotangent[...], order, TN)
    total = dot(pair[...], order, TN)
    for t in range(2):
        scaled, inverse = norm(take(got, t))
        gain_t = column(gates[256 + t : 257 + t])
        normed = (scaled * gain_t).astype(BF)
        gate = gates[128 * t : 128 * t + 128]
        final = dot(w_final[t], normed, TN)
        total = total + gate * final
        grad_final = (upstream * gate).astype(BF)
        grad_gate[128 * t : 128 * t + 128] = (upstream * final * gate * (1.0 - gate)).astype(BF)
        weighted = dot(w_final[t], grad_final) * gain_t
        send[:, 8 * t : 8 * t + 8] = groups(norm_back(weighted, scaled, inverse))
    updated[...] = dot(order, total.astype(BF), NT).astype(BF)


def last_kernel(cotangent, got, proj, grad_gate, scaled_t, w_out, w_in, w_gate, grad_pair):
    order = pair_order()
    upstream = dot(cotangent[...], order, TN)
    grad_normed = dot(w_gate[...], grad_gate[...])
    for half, weights in enumerate((w_out, w_in)):
        p = proj[half]
        parts = []
        for side in range(2):
            grad = take(got, 2 * half + side)
            sig = jax.nn.sigmoid(p[256 * side : 256 * side + 128])
            parts.append(grad * p[256 * side + 128 : 256 * side + 256] * sig * (1.0 - sig))
            parts.append(grad * sig)
        grad_normed = grad_normed + dot(
            weights[...], jnp.concatenate(parts, axis=0).astype(BF)
        )
    weighted = grad_normed * column(scaled_t[129:130])
    back = norm_back(weighted, scaled_t[0:128], scaled_t[128:129])
    grad_pair[...] = dot(order, (upstream + back).astype(BF), NT).astype(BF)


def call(kernel, out, *args, scratch=(), spot=False, far=()):
    specs = [pl.BlockSpec(memory_space=pltpu.VMEM)] * len(args)
    for n in far:
        specs[n] = pl.BlockSpec(memory_space=pl.ANY)
    if spot:
        specs[0] = pl.BlockSpec(memory_space=pltpu.SMEM)
    multi = isinstance(out, list)
    shapes = [jax.ShapeDtypeStruct(s, d) for s, d in (out if multi else [out])]
    outs = [pl.BlockSpec(memory_space=pltpu.VMEM)] * len(shapes)
    buffers = [pltpu.VMEM(args[n].shape, args[n].dtype) for n in far]
    buffers += [pltpu.VMEM(s, F32) for s in scratch]
    if far:
        buffers.append(pltpu.SemaphoreType.DMA((len(far),)))
    params = pltpu.CompilerParams(vmem_limit_bytes=32 * 1024 * 1024)
    if len(far) == len(args):
        params = None
    result = pl.pallas_call(
        kernel,
        out_shape=shapes,
        in_specs=specs,
        out_specs=outs,
        scratch_shapes=buffers,
        compiler_params=params,
    )(*args)
    return result if multi else result[0]


def exchange(values, axis):
    return lax.all_to_all(values, axis, 0, 0, tiled=True)


def to_channels(send, full, parts):
    spread = call(
        functools.partial(spread_kernel, full, parts),
        ((8, 4, 32, 128), BF),
        exchange(send, DEPTH),
        scratch=[(8, 16, 128), (8, 4, 16, 128)],
    )
    return exchange(spread.reshape(32, 32, 128), PLANE).reshape(4, 8, 32, 128)


def to_pairs(send, full, parts):
    rows = 8 + 8 * len(parts)
    back = call(
        functools.partial(collect_kernel, full, parts),
        ((16, rows, 128), BF),
        exchange(send.reshape(32, 32, 128), PLANE).reshape(8, 4, 32, 128),
        scratch=[(8, 16, 128), (8, 4, 16, 128), (16, rows, 128)],
    )
    return exchange(back, DEPTH)


def my_mate():
    return lax.axis_index(PLANE) & 3


def on_device(
    pair_rep, cotangent, contact, norm_gain, w_out_proj, w_in_proj, update_gain, w_gate, w_final
):
    pair = pair_rep.reshape(128, 128)
    upstream = cotangent.reshape(128, 128)
    mate = my_mate().reshape(1)
    flat = contact.reshape(256, 16)

    send, proj, gates, scaled_t = call(
        first_kernel,
        [
            ((16, 32, 128), BF),
            ((2, 512, 128), F32),
            ((264, 128), F32),
            ((136, 128), F32),
        ],
        pair,
        norm_gain.reshape(1, 128),
        w_out_proj,
        w_in_proj,
        w_gate,
        update_gain,
        far=range(6),
    )
    sides = to_channels(send, 1, (0, 2, 3, 1))
    triangles = call(
        forward_kernel,
        ((4, 8, 32, 128), BF),
        mate,
        sides,
        contact,
        flat,
        scratch=[(16, 256)],
        spot=True,
        far=(2,),
    )
    updated, send, grad_gate = call(
        middle_kernel,
        [((128, 128), BF), ((16, 16, 128), BF), ((256, 128), BF)],
        pair,
        upstream,
        to_pairs(triangles, 1, (0,)),
        gates,
        w_final,
    )
    grads = call(
        backward_kernel,
        ((4, 8, 32, 128), BF),
        mate,
        sides,
        to_channels(send, 1, (0, 0, 0, 0)),
        contact,
        flat,
        scratch=[(16, 256)],
        spot=True,
        far=(3,),
    )
    grad_pair = call(
        last_kernel,
        ((128, 128), BF),
        upstream,
        to_pairs(grads, 1, (0, 2, 3)),
        proj,
        grad_gate,
        scaled_t,
        w_out_proj,
        w_in_proj,
        w_gate,
    )
    return (updated.reshape(pair_rep.shape), grad_pair.reshape(pair_rep.shape))


def solution(mesh):
    fine = Mesh(mesh.devices.reshape(4, 4, 4, 4, 2), ("zl", "x", "y", "zh", "core"))
    block = P(("zl", "x"), ("y", "zh", "core"), None)
    in_specs = (block, block, P(), P(), P(), P(), P(), P(), P())
    return jax.shard_map(
        on_device, mesh=fine, in_specs=in_specs, out_specs=(block, block), check_vma=False
    )
```

```python
import functools

import jax
import jax.numpy as jnp
from jax import lax
from jax.experimental import pallas as pl
from jax.experimental.pallas import tpu as pltpu
from jax.sharding import Mesh
from jax.sharding import PartitionSpec as P


PLANE = ("x", "y", "core")
DEPTH = ("zl", "zh")
EPSILON = 1e-05
BF = jnp.bfloat16
F32 = jnp.float32


def dot(a, b, dims=((1,), (0,))):
    return lax.dot_general(a, b, (dims, ((), ())), preferred_element_type=F32)


def norm(values):
    center = jnp.mean(values, axis=0, keepdims=True)
    shifted = values - center
    inverse = lax.rsqrt(jnp.mean(shifted * shifted, axis=0, keepdims=True) + EPSILON)
    return shifted * inverse, inverse


def norm_back(weighted, scaled, inverse):
    first = jnp.mean(weighted, axis=0, keepdims=True)
    second = jnp.mean(weighted * scaled, axis=0, keepdims=True)
    return inverse * (weighted - first - scaled * second)


def pair_order():
    here = lax.broadcasted_iota(jnp.int32, (128, 128), 0)
    there = lax.broadcasted_iota(jnp.int32, (128, 128), 1)
    same = (here >> 3 == (there & 15)) & ((here & 7) == there >> 4)
    return same.astype(F32).astype(BF)


def column(gain):
    return jnp.broadcast_to(gain, (128, 128)).T


def groups(values):
    return values.reshape(16, 8, 128).astype(BF)


def take(got, array):
    return got[:, 8 * array : 8 * array + 8].astype(F32).reshape(128, 128)


def fetch(pairs, arrived):
    copies = [
        pltpu.make_async_copy(there, here, arrived.at[n]) for n, (there, here) in enumerate(pairs)
    ]
    for copy in copies:
        copy.start()
    return copies


def first_kernel(*refs):
    spot, far, near = refs[0], refs[1:7], refs[12:18]
    send, proj, gates, scaled_t, mate = refs[7:12]
    copies = fetch(list(zip(far, near)), refs[18])
    mate[0] = spot[0]
    pair, gain, w_out, w_in, w_gate, update = near
    copies[0].wait()
    pair_t = dot(pair[...], pair_order(), ((0,), (0,)))
    scaled, inverse = norm(pair_t)
    copies[1].wait()
    normed = (scaled * column(gain[...])).astype(BF)
    scaled_t[0:128] = scaled
    scaled_t[128:129] = inverse
    scaled_t[129:130] = gain[...]
    for half, weights in enumerate((w_out, w_in)):
        copies[2 + half].wait()
        p = dot(weights[...], normed, ((0,), (0,)))
        proj[half] = p
        for side in range(2):
            part = 256 * side
            gated = jax.nn.sigmoid(p[part : part + 128]) * p[part + 128 : part + 256]
            row = 16 * half + 8 * side
            send[:, row : row + 8] = groups(gated)
    copies[4].wait()
    copies[5].wait()
    gates[0:256] = jax.nn.sigmoid(dot(w_gate[...], normed, ((0,), (0,))))
    gates[256:258] = update[...]


def swap_groups(rows):
    rows = list(rows)
    group = lax.broadcasted_iota(jnp.int32, rows[0].shape, 1) >> 4
    step = len(rows) // 2
    while step:
        low = (group & step) == 0
        for a in range(len(rows)):
            if a & step:
                continue
            x, y = rows[a], rows[a + step]
            rows[a] = jnp.where(low, x, pltpu.roll(y, 16 * step, 1))
            rows[a + step] = jnp.where(low, pltpu.roll(x, 128 - 16 * step, 1), y)
        step //= 2
    return rows


def spread_kernel(full, parts, got, send, held_full, held_parts):
    for high in range(2):
        rows = swap_groups(
            [got[4 * zl + 2 * high + low].astype(F32) for low in range(2) for zl in range(4)]
        )
        for q in range(8):
            held_full[:, 8 * high + q] = rows[q][8 * full : 8 * full + 8]
            pieces = swap_groups([rows[q][8 * a : 8 * a + 8] for a in parts])
            for mate in range(4):
                held_parts[:, mate, 8 * high + q] = pieces[mate]
    values = held_full[...].astype(BF)
    for mate in range(4):
        send[:, mate, 0:16] = values
    send[:, :, 16:32] = held_parts[...].astype(BF)


def collect_kernel(full, parts, got, send, held, held_parts, out):
    values = got[...].astype(F32)
    held[...] = values[:, 0, 0:16] + values[:, 1, 0:16] + values[:, 2, 0:16] + values[:, 3, 0:16]
    held_parts[...] = values[:, :, 16:32]
    for high in range(2):
        by_q = []
        for q in range(8):
            row = 8 * high + q
            pieces = swap_groups([held_parts[:, mate, row] for mate in range(4)])
            by_q.append({full: held[:, row], **dict(zip(parts, pieces))})
        for a in (full, *parts):
            for g, rows in enumerate(swap_groups([by_q[q][a] for q in range(8)])):
                zh = 2 * high + (g >> 2)
                out[4 * (g & 3) + zh, 8 * a : 8 * a + 8] = rows
    send[...] = out[...].astype(BF)


def swap_halves(first, second):
    low = lax.broadcasted_iota(jnp.int32, first.shape, 1) < 64
    return (
        jnp.where(low, first, pltpu.roll(second, 64, 1)),
        jnp.where(low, pltpu.roll(first, 64, 1), second),
    )


def reorder():
    p = lax.broadcasted_iota(jnp.int32, (256, 256), 0)
    q = lax.broadcasted_iota(jnp.int32, (256, 256), 1)
    residue = ((p >> 4) & 3) * 64 + (p >> 6) * 16 + (p & 15)
    return one_hot(residue, q_block(q) * 16 + ((q >> 4) & 1) * 8 + (q & 7))


def whole(got):
    tiles = [got[x, :, 0:16].astype(F32).reshape(128, 128) for x in range(4)]
    left = swap_halves(tiles[0], tiles[1])
    right = swap_halves(tiles[2], tiles[3])
    values = jnp.concatenate(
        [jnp.concatenate([left[low], right[low]], axis=1) for low in range(2)], axis=0
    )
    return dot(values.astype(BF), reorder())


def quarters(got, amount):
    tiles = [got[x, :, 16:32].astype(F32).reshape(128, 128) for x in range(4)]
    turned = [values.T for values in swap_groups(tiles)[:amount]]
    return [jnp.concatenate([t[0:64], t[64:128]], axis=1).astype(BF) for t in turned]


def send_whole(send, values):
    values = dot(values.astype(BF), reorder(), NT)
    for half in range(2):
        lanes = slice(128 * half, 128 * half + 128)
        tiles = swap_halves(values[0:128, lanes], values[128:256, lanes])
        for n in range(2):
            send[2 * half + n, :, 0:16] = tiles[n].reshape(8, 16, 128).astype(BF)


def send_quarters(send, arrays):
    rows = []
    for pieces in arrays:
        values = jnp.concatenate(pieces, axis=0)
        rows.append(jnp.concatenate([values[:, 0:128], values[:, 128:256]], axis=0).T)
    while len(rows) < 4:
        rows.append(jnp.zeros((128, 128), F32))
    for x, tile in enumerate(swap_groups(rows)):
        send[x, :, 16:32] = tile.reshape(8, 16, 128).astype(BF)


NN = ((1,), (0,))
NT = ((1,), (1,))
TN = ((0,), (0,))


def one_hot(label, values):
    return (label == values).astype(F32).astype(BF)


def q_block(place):
    return ((place >> 5) & 3) * 4 + ((place >> 3) & 1) * 2 + (place >> 7)


def masks(contact, flat, mate):
    place = lax.broadcasted_iota(jnp.int32, (32, 16), 0) << 3
    label = lax.broadcasted_iota(jnp.int32, (32, 16), 1)
    short = one_hot(label, q_block(place))
    place = lax.broadcasted_iota(jnp.int32, (256, 16), 0)
    label = lax.broadcasted_iota(jnp.int32, (256, 16), 1)
    table = one_hot(label, q_block(place))
    place = lax.broadcasted_iota(jnp.int32, (32, 256), 0) << 3
    label = lax.broadcasted_iota(jnp.int32, (32, 256), 1)
    j_short = (label & 15 == q_block(place)).astype(F32)
    place = lax.broadcasted_iota(jnp.int32, (256, 256), 0)
    label = lax.broadcasted_iota(jnp.int32, (256, 256), 1)
    i_table = one_hot(label >> 4, q_block(place))
    by_k = flat[...].astype(F32)
    wanted = lax.broadcasted_iota(jnp.int32, (4, 16), 0) + 4 * mate
    label = lax.broadcasted_iota(jnp.int32, (4, 16), 1)
    by_k = dot(one_hot(label, wanted), by_k.astype(BF), NT)
    for_out = [
        dot(short, contact[4 * mate + t].astype(F32).astype(BF), NT).astype(BF) for t in range(4)
    ]
    for_in = [(j_short * by_k[t : t + 1]).astype(BF) for t in range(4)]
    mask_out = dot(jnp.concatenate(for_out, axis=0), table, NT)
    mask_in = dot(jnp.concatenate(for_in, axis=0), i_table, NT)
    return mask_out.reshape(4, 32, 1, 256), mask_in.reshape(4, 32, 1, 256)


def apply(mask, values):
    return (values.reshape(32, 8, 256) * mask).reshape(256, 256)


def forward_kernel(spot, got, contact, flat, send, near, arrived):
    copies = fetch([(contact, near)], arrived)
    right_out = whole(got)
    left_out, left_in, right_in = quarters(got, 3)
    copies[0].wait()
    mask_out, mask_in = masks(near, flat, spot[0])
    outs, ins = [], None
    for t in range(4):
        part = slice(16 * t, 16 * t + 16)
        outs.append(dot(left_out[part], apply(mask_out[t], right_out).astype(BF), NN))
        term = apply(mask_in[t], dot(right_in[part], left_in[part], TN))
        ins = term if ins is None else ins + term
    send_whole(send, ins)
    send_quarters(send, [outs])


def backward_kernel(spot, got, grads, contact, flat, send, near, arrived):
    copies = fetch([(contact, near)], arrived)
    right_out = whole(got)
    left_out, left_in, right_in = quarters(got, 3)
    grad_in = whole(grads)
    grad_out = quarters(grads, 1)[0]
    copies[0].wait()
    mask_out, mask_in = masks(near, flat, spot[0])
    grad_left_out, grad_left_in, grad_right_in, grad_right_out = [], [], [], None
    for t in range(4):
        part = slice(16 * t, 16 * t + 16)
        grad_left_out.append(dot(grad_out[part], apply(mask_out[t], right_out).astype(BF), NT))
        term = apply(mask_out[t], dot(left_out[part], grad_out[part], TN))
        grad_right_out = term if grad_right_out is None else grad_right_out + term
        both = apply(mask_in[t], grad_in).astype(BF)
        grad_left_in.append(dot(right_in[part], both, NN))
        grad_right_in.append(dot(left_in[part], both, NT))
    send_whole(send, grad_right_out)
    send_quarters(send, [grad_left_out, grad_left_in, grad_right_in])


def middle_kernel(pair, cotangent, got, gates, w_final, updated, send, grad_gate):
    order = pair_order()
    upstream = dot(cotangent[...], order, TN)
    total = dot(pair[...], order, TN)
    for t in range(2):
        scaled, inverse = norm(take(got, t))
        gain_t = column(gates[256 + t : 257 + t])
        normed = (scaled * gain_t).astype(BF)
        gate = gates[128 * t : 128 * t + 128]
        final = dot(w_final[t], normed, TN)
        total = total + gate * final
        grad_final = (upstream * gate).astype(BF)
        grad_gate[128 * t : 128 * t + 128] = (upstream * final * gate * (1.0 - gate)).astype(BF)
        weighted = dot(w_final[t], grad_final) * gain_t
        send[:, 8 * t : 8 * t + 8] = groups(norm_back(weighted, scaled, inverse))
    updated[...] = dot(order, total.astype(BF), NT).astype(BF)


def last_kernel(cotangent, got, proj, grad_gate, scaled_t, w_out, w_in, w_gate, grad_pair):
    order = pair_order()
    upstream = dot(cotangent[...], order, TN)
    grad_normed = dot(w_gate[...], grad_gate[...])
    for half, weights in enumerate((w_out, w_in)):
        p = proj[half]
        parts = []
        for side in range(2):
            grad = take(got, 2 * half + side)
            sig = jax.nn.sigmoid(p[256 * side : 256 * side + 128])
            parts.append(grad * p[256 * side + 128 : 256 * side + 256] * sig * (1.0 - sig))
            parts.append(grad * sig)
        grad_normed = grad_normed + dot(
            weights[...], jnp.concatenate(parts, axis=0).astype(BF)
        )
    weighted = grad_normed * column(scaled_t[129:130])
    back = norm_back(weighted, scaled_t[0:128], scaled_t[128:129])
    grad_pair[...] = dot(order, (upstream + back).astype(BF), NT).astype(BF)


def call(kernel, out, *args, scratch=(), spot=False, far=()):
    specs = [pl.BlockSpec(memory_space=pltpu.VMEM)] * len(args)
    for n in far:
        specs[n] = pl.BlockSpec(memory_space=pltpu.HBM)
    if spot:
        specs[0] = pl.BlockSpec(memory_space=pltpu.SMEM)
    multi = isinstance(out, list)
    shapes = [jax.ShapeDtypeStruct(s, d) for s, d in (out if multi else [out])]
    outs = [
        pl.BlockSpec(memory_space=pltpu.SMEM if x.dtype == jnp.int32 else pltpu.VMEM)
        for x in shapes
    ]
    buffers = [pltpu.VMEM(args[n].shape, args[n].dtype) for n in far]
    buffers += [pltpu.VMEM(s, F32) for s in scratch]
    if far:
        buffers.append(pltpu.SemaphoreType.DMA((len(far),)))
    params = pltpu.CompilerParams(vmem_limit_bytes=32 * 1024 * 1024)
    result = pl.pallas_call(
        kernel,
        out_shape=shapes,
        in_specs=specs,
        out_specs=outs,
        scratch_shapes=buffers,
        compiler_params=params,
    )(*args)
    return result if multi else result[0]


def exchange(values, axis):
    return lax.all_to_all(values, axis, 0, 0, tiled=True)


def to_channels(send, full, parts):
    spread = call(
        functools.partial(spread_kernel, full, parts),
        ((8, 4, 32, 128), BF),
        exchange(send, DEPTH),
        scratch=[(8, 16, 128), (8, 4, 16, 128)],
    )
    return exchange(spread.reshape(32, 32, 128), PLANE).reshape(4, 8, 32, 128)


def to_pairs(send, full, parts):
    rows = 8 + 8 * len(parts)
    back = call(
        functools.partial(collect_kernel, full, parts),
        ((16, rows, 128), BF),
        exchange(send.reshape(32, 32, 128), PLANE).reshape(8, 4, 32, 128),
        scratch=[(8, 16, 128), (8, 4, 16, 128), (16, rows, 128)],
    )
    return exchange(back, DEPTH)


def my_mate():
    return lax.axis_index(PLANE) & 3


def on_device(
    pair_rep, cotangent, contact, norm_gain, w_out_proj, w_in_proj, update_gain, w_gate, w_final
):
    pair = pair_rep.reshape(128, 128)
    upstream = cotangent.reshape(128, 128)
    flat = contact.reshape(256, 16)

    send, proj, gates, scaled_t, mate = call(
        first_kernel,
        [
            ((16, 32, 128), BF),
            ((2, 512, 128), F32),
            ((264, 128), F32),
            ((136, 128), F32),
            ((1,), jnp.int32),
        ],
        my_mate().reshape(1),
        pair,
        norm_gain.reshape(1, 128),
        w_out_proj,
        w_in_proj,
        w_gate,
        update_gain,
        spot=True,
        far=range(1, 7),
    )
    sides = to_channels(send, 1, (0, 2, 3, 1))
    triangles = call(
        forward_kernel,
        ((4, 8, 32, 128), BF),
        mate,
        sides,
        contact,
        flat,
        spot=True,
        far=(2,),
    )
    updated, send, grad_gate = call(
        middle_kernel,
        [((128, 128), BF), ((16, 16, 128), BF), ((256, 128), BF)],
        pair,
        upstream,
        to_pairs(triangles, 1, (0,)),
        gates,
        w_final,
    )
    grads = call(
        backward_kernel,
        ((4, 8, 32, 128), BF),
        mate,
        sides,
        to_channels(send, 1, (0, 0, 0, 0)),
        contact,
        flat,
        spot=True,
        far=(3,),
    )
    grad_pair = call(
        last_kernel,
        ((128, 128), BF),
        upstream,
        to_pairs(grads, 1, (0, 2, 3)),
        proj,
        grad_gate,
        scaled_t,
        w_out_proj,
        w_in_proj,
        w_gate,
    )
    return (updated.reshape(pair_rep.shape), grad_pair.reshape(pair_rep.shape))


def solution(mesh):
    fine = Mesh(mesh.devices.reshape(4, 4, 4, 4, 2), ("zl", "x", "y", "zh", "core"))
    block = P(("zl", "x"), ("y", "zh", "core"), None)
    in_specs = (block, block, P(), P(), P(), P(), P(), P(), P())
    return jax.shard_map(
        on_device, mesh=fine, in_specs=in_specs, out_specs=(block, block), check_vma=False
    )
```

```python
import functools

import jax
import jax.numpy as jnp
from jax import lax
from jax.experimental import pallas as pl
from jax.experimental.pallas import tpu as pltpu
from jax.sharding import Mesh
from jax.sharding import PartitionSpec as P


PLANE = ("x", "y", "core")
DEPTH = ("zl", "zh")
EPSILON = 1e-05
BF = jnp.bfloat16
F32 = jnp.float32


def dot(a, b, dims=((1,), (0,))):
    return lax.dot_general(a, b, (dims, ((), ())), preferred_element_type=F32)


def norm(values):
    center = jnp.mean(values, axis=0, keepdims=True)
    shifted = values - center
    inverse = lax.rsqrt(jnp.mean(shifted * shifted, axis=0, keepdims=True) + EPSILON)
    return shifted * inverse, inverse


def norm_back(weighted, scaled, inverse):
    first = jnp.mean(weighted, axis=0, keepdims=True)
    second = jnp.mean(weighted * scaled, axis=0, keepdims=True)
    return inverse * (weighted - first - scaled * second)


def pair_order():
    here = lax.broadcasted_iota(jnp.int32, (128, 128), 0)
    there = lax.broadcasted_iota(jnp.int32, (128, 128), 1)
    same = (here >> 3 == (there & 15)) & ((here & 7) == there >> 4)
    return same.astype(F32).astype(BF)


def column(gain):
    return jnp.broadcast_to(gain, (128, 128)).T


def groups(values):
    return values.reshape(16, 8, 128).astype(BF)


def take(got, array):
    return got[:, 8 * array : 8 * array + 8].astype(F32).reshape(128, 128)


def fetch(pairs, arrived):
    copies = [
        pltpu.make_async_copy(there, here, arrived.at[n]) for n, (there, here) in enumerate(pairs)
    ]
    for copy in copies:
        copy.start()
    return copies


def first_kernel(*refs):
    spot, far, near = refs[0], refs[1:7], refs[12:18]
    send, proj, gates, scaled_t, mate = refs[7:12]
    copies = fetch(list(zip(far, near)), refs[18])
    mate[0] = spot[0]
    pair, gain, w_out, w_in, w_gate, update = near
    copies[0].wait()
    pair_t = dot(pair[...], pair_order(), ((0,), (0,)))
    scaled, inverse = norm(pair_t)
    copies[1].wait()
    normed = (scaled * column(gain[...])).astype(BF)
    scaled_t[0:128] = scaled
    scaled_t[128:129] = inverse
    scaled_t[129:130] = gain[...]
    for half, weights in enumerate((w_out, w_in)):
        copies[2 + half].wait()
        p = dot(weights[...], normed, ((0,), (0,)))
        proj[half] = p
        for side in range(2):
            part = 256 * side
            gated = jax.nn.sigmoid(p[part : part + 128]) * p[part + 128 : part + 256]
            row = 16 * half + 8 * side
            send[:, row : row + 8] = groups(gated)
    copies[4].wait()
    copies[5].wait()
    gates[0:256] = jax.nn.sigmoid(dot(w_gate[...], normed, ((0,), (0,))))
    gates[256:258] = update[...]


def swap_groups(rows):
    rows = list(rows)
    group = lax.broadcasted_iota(jnp.int32, rows[0].shape, 1) >> 4
    step = len(rows) // 2
    while step:
        low = (group & step) == 0
        for a in range(len(rows)):
            if a & step:
                continue
            x, y = rows[a], rows[a + step]
            rows[a] = jnp.where(low, x, pltpu.roll(y, 16 * step, 1))
            rows[a + step] = jnp.where(low, pltpu.roll(x, 128 - 16 * step, 1), y)
        step //= 2
    return rows


def spread_kernel(full, parts, got, send, held_full, held_parts):
    pieces = []
    for high in range(2):
        rows = swap_groups(
            [got[4 * zl + 2 * high + low].astype(F32) for low in range(2) for zl in range(4)]
        )
        for q in range(8):
            held_full[:, 8 * high + q] = rows[q][8 * full : 8 * full + 8]
            pieces.append([rows[q][8 * a : 8 * a + 8] for a in parts])
    if len(parts) == 1:
        pieces = [pieces[q] + pieces[8 + q] for q in range(8)]
    for row, arrays in enumerate(pieces):
        for mate, values in enumerate(swap_groups(arrays + arrays[: 4 - len(arrays)])):
            held_parts[:, mate, row] = values
    values = held_full[...].astype(BF)
    for mate in range(4):
        send[:, mate, 0:16] = values
    send[:, :, 16:] = held_parts[...].astype(BF)


def collect_kernel(full, parts, got, send, held, held_parts, out):
    values = got[...].astype(F32)
    held[...] = values[:, 0, 0:16] + values[:, 1, 0:16] + values[:, 2, 0:16] + values[:, 3, 0:16]
    held_parts[...] = values[:, :, 16:]
    pieces = [
        swap_groups([held_parts[:, mate, row] for mate in range(4)])
        for row in range(got.shape[2] - 16)
    ]
    if len(parts) == 1:
        pieces = [[values[high]] for high in range(2) for values in pieces]
    for high in range(2):
        arrays = {full: [held[:, 8 * high + q] for q in range(8)]}
        for n, a in enumerate(parts):
            arrays[a] = [pieces[8 * high + q][n] for q in range(8)]
        for a, rows in arrays.items():
            for g, values in enumerate(swap_groups(rows)):
                zh = 2 * high + (g >> 2)
                out[4 * (g & 3) + zh, 8 * a : 8 * a + 8] = values
    send[...] = out[...].astype(BF)


def swap_halves(first, second):
    low = lax.broadcasted_iota(jnp.int32, first.shape, 1) < 64
    return (
        jnp.where(low, first, pltpu.roll(second, 64, 1)),
        jnp.where(low, pltpu.roll(first, 64, 1), second),
    )


def p_block(place):
    return ((place >> 4) & 3) * 4 + (place >> 6)


def reorder(turned=False):
    p = lax.broadcasted_iota(jnp.int32, (256, 256), 1 if turned else 0)
    q = lax.broadcasted_iota(jnp.int32, (256, 256), 0 if turned else 1)
    residue = p_block(p) * 16 + (p & 15)
    return one_hot(residue, q_block(q) * 16 + ((q >> 4) & 1) * 8 + (q & 7))


def whole(got, order):
    tiles = [got[x, :, 0:16].astype(F32).reshape(128, 128) for x in range(4)]
    left = swap_halves(tiles[0], tiles[1])
    right = swap_halves(tiles[2], tiles[3])
    values = jnp.concatenate(
        [jnp.concatenate([left[low], right[low]], axis=1) for low in range(2)], axis=0
    )
    return dot(values.astype(BF), order)


def quarters(got):
    rows = got.shape[2] - 16
    tiles = [got[x, :, 16:].astype(F32).reshape(8 * rows, 128) for x in range(4)]
    arrays = swap_groups(tiles)
    if rows == 8:
        highs = [values.reshape(8, 1, 8, 128) for values in arrays[:2]]
        arrays = [jnp.concatenate(highs, axis=1).reshape(128, 128)]
    turned = [values.T for values in arrays[:3]]
    return [jnp.concatenate([t[0:64], t[64:128]], axis=1).astype(BF) for t in turned]


def send_whole(send, values, back):
    values = dot(values.astype(BF), back)
    for half in range(2):
        lanes = slice(128 * half, 128 * half + 128)
        tiles = swap_halves(values[0:128, lanes], values[128:256, lanes])
        for n in range(2):
            send[2 * half + n, :, 0:16] = tiles[n].reshape(8, 16, 128).astype(BF)


def send_quarters(send, arrays):
    rows = [
        jnp.concatenate([values[:, 0:128], values[:, 128:256]], axis=0).T for values in arrays
    ]
    if len(rows) == 1:
        highs = rows[0].reshape(8, 2, 8, 128)
        rows = [highs[:, n].reshape(64, 128) for n in range(2)]
    rows += rows[: 4 - len(rows)]
    for x, tile in enumerate(swap_groups(rows)):
        send[x, :, 16:] = tile.reshape(8, send.shape[2] - 16, 128).astype(BF)


NN = ((1,), (0,))
NT = ((1,), (1,))
TN = ((0,), (0,))


def one_hot(label, values):
    return (label == values).astype(F32).astype(BF)


def q_block(place):
    return ((place >> 5) & 3) * 4 + ((place >> 3) & 1) * 2 + (place >> 7)


def masks(contact, flat, mate):
    place = lax.broadcasted_iota(jnp.int32, (32, 16), 0) << 3
    label = lax.broadcasted_iota(jnp.int32, (32, 16), 1)
    short = one_hot(label, q_block(place))
    place = lax.broadcasted_iota(jnp.int32, (256, 16), 0)
    label = lax.broadcasted_iota(jnp.int32, (256, 16), 1)
    table = one_hot(label, q_block(place))
    place = lax.broadcasted_iota(jnp.int32, (32, 256), 0) << 3
    label = lax.broadcasted_iota(jnp.int32, (32, 256), 1)
    j_short = (label & 15 == q_block(place)).astype(F32)
    place = lax.broadcasted_iota(jnp.int32, (256, 256), 0)
    label = lax.broadcasted_iota(jnp.int32, (256, 256), 1)
    i_table = one_hot(label >> 4, q_block(place))
    by_k = flat[...].astype(F32)
    wanted = lax.broadcasted_iota(jnp.int32, (4, 16), 0) + 4 * mate
    label = lax.broadcasted_iota(jnp.int32, (4, 16), 1)
    by_k = dot(one_hot(label, wanted), by_k.astype(BF), NT)
    for_out = [
        dot(short, contact[4 * mate + t].astype(F32).astype(BF), NT).astype(BF) for t in range(4)
    ]
    for_in = [(j_short * by_k[t : t + 1]).astype(BF) for t in range(4)]
    mask_out = dot(jnp.concatenate(for_out, axis=0), table, NT)
    mask_in = dot(jnp.concatenate(for_in, axis=0), i_table, NT)
    return mask_out.reshape(4, 32, 1, 256), mask_in.reshape(4, 32, 1, 256)


def apply(mask, values):
    return (values.reshape(32, 8, 256) * mask).reshape(256, 256)


def join(pieces):
    return jnp.concatenate(pieces, axis=0)


def forward_kernel(spot, got, contact, flat, send, near, arrived):
    copies = fetch([(contact, near)], arrived)
    order, back = reorder(), reorder(True)
    left_out, left_in, right_in = quarters(got)
    right_out = whole(got, order)
    copies[0].wait()
    mask_out, mask_in = masks(near, flat, spot[0])
    outs, ins = [], None
    for t in range(4):
        part = slice(16 * t, 16 * t + 16)
        outs.append(dot(left_out[part], apply(mask_out[t], right_out).astype(BF), NN))
        term = apply(mask_in[t], dot(right_in[part], left_in[part], TN))
        ins = term if ins is None else ins + term
    send_whole(send, ins, back)
    send_quarters(send, [join(outs)])


def backward_kernel(spot, got, grads, contact, flat, send, near, arrived):
    copies = fetch([(contact, near)], arrived)
    order, back = reorder(), reorder(True)
    left_out, left_in, right_in = quarters(got)
    grad_out = quarters(grads)[0]
    right_out = whole(got, order)
    grad_in = whole(grads, order)
    copies[0].wait()
    mask_out, mask_in = masks(near, flat, spot[0])
    grad_left_out, grad_left_in, grad_right_in, grad_right_out = [], [], [], None
    for t in range(4):
        part = slice(16 * t, 16 * t + 16)
        grad_left_out.append(dot(grad_out[part], apply(mask_out[t], right_out).astype(BF), NT))
        term = apply(mask_out[t], dot(left_out[part], grad_out[part], TN))
        grad_right_out = term if grad_right_out is None else grad_right_out + term
        both = apply(mask_in[t], grad_in).astype(BF)
        grad_left_in.append(dot(right_in[part], both, NN))
        grad_right_in.append(dot(left_in[part], both, NT))
    send_whole(send, grad_right_out, back)
    send_quarters(send, [join(grad_left_out), join(grad_left_in), join(grad_right_in)])


def middle_kernel(pair, cotangent, got, gates, w_final, updated, send, grad_gate):
    order = pair_order()
    upstream = dot(cotangent[...], order, TN)
    total = dot(pair[...], order, TN)
    for t in range(2):
        scaled, inverse = norm(take(got, t))
        gain_t = column(gates[256 + t : 257 + t])
        normed = (scaled * gain_t).astype(BF)
        gate = gates[128 * t : 128 * t + 128]
        final = dot(w_final[t], normed, TN)
        total = total + gate * final
        grad_final = (upstream * gate).astype(BF)
        grad_gate[128 * t : 128 * t + 128] = (upstream * final * gate * (1.0 - gate)).astype(BF)
        weighted = dot(w_final[t], grad_final) * gain_t
        send[:, 8 * t : 8 * t + 8] = groups(norm_back(weighted, scaled, inverse))
    updated[...] = dot(order, total.astype(BF), NT).astype(BF)


def last_kernel(cotangent, got, proj, grad_gate, scaled_t, w_out, w_in, w_gate, grad_pair):
    order = pair_order()
    upstream = dot(cotangent[...], order, TN)
    grad_normed = dot(w_gate[...], grad_gate[...])
    for half, weights in enumerate((w_out, w_in)):
        p = proj[half]
        parts = []
        for side in range(2):
            grad = take(got, 2 * half + side)
            sig = jax.nn.sigmoid(p[256 * side : 256 * side + 128])
            parts.append(grad * p[256 * side + 128 : 256 * side + 256] * sig * (1.0 - sig))
            parts.append(grad * sig)
        grad_normed = grad_normed + dot(
            weights[...], jnp.concatenate(parts, axis=0).astype(BF)
        )
    weighted = grad_normed * column(scaled_t[129:130])
    back = norm_back(weighted, scaled_t[0:128], scaled_t[128:129])
    grad_pair[...] = dot(order, (upstream + back).astype(BF), NT).astype(BF)


def call(kernel, out, *args, scratch=(), spot=False, far=()):
    specs = [pl.BlockSpec(memory_space=pltpu.VMEM)] * len(args)
    for n in far:
        specs[n] = pl.BlockSpec(memory_space=pltpu.HBM)
    if spot:
        specs[0] = pl.BlockSpec(memory_space=pltpu.SMEM)
    multi = isinstance(out, list)
    shapes = [jax.ShapeDtypeStruct(s, d) for s, d in (out if multi else [out])]
    outs = [
        pl.BlockSpec(memory_space=pltpu.SMEM if x.dtype == jnp.int32 else pltpu.VMEM)
        for x in shapes
    ]
    buffers = [pltpu.VMEM(args[n].shape, args[n].dtype) for n in far]
    buffers += [pltpu.VMEM(s, F32) for s in scratch]
    if far:
        buffers.append(pltpu.SemaphoreType.DMA((len(far),)))
    params = pltpu.CompilerParams(vmem_limit_bytes=32 * 1024 * 1024)
    if len(far) > 1:
        params = None
    result = pl.pallas_call(
        kernel,
        out_shape=shapes,
        in_specs=specs,
        out_specs=outs,
        scratch_shapes=buffers,
        compiler_params=params,
    )(*args)
    return result if multi else result[0]


def exchange(values, axis):
    return lax.all_to_all(values, axis, 0, 0, tiled=True)


def to_channels(send, full, parts):
    rows = 24 if len(parts) == 1 else 32
    spread = call(
        functools.partial(spread_kernel, full, parts),
        ((8, 4, rows, 128), BF),
        exchange(send, DEPTH),
        scratch=[(8, 16, 128), (8, 4, rows - 16, 128)],
    )
    return exchange(spread.reshape(32, rows, 128), PLANE).reshape(4, 8, rows, 128)


def to_pairs(send, full, parts):
    rows = send.shape[2]
    amount = 8 + 8 * len(parts)
    back = call(
        functools.partial(collect_kernel, full, parts),
        ((16, amount, 128), BF),
        exchange(send.reshape(32, rows, 128), PLANE).reshape(8, 4, rows, 128),
        scratch=[(8, 16, 128), (8, 4, rows - 16, 128), (16, amount, 128)],
    )
    return exchange(back, DEPTH)


def my_mate():
    return lax.axis_index(PLANE) & 3


def on_device(
    pair_rep, cotangent, contact, norm_gain, w_out_proj, w_in_proj, update_gain, w_gate, w_final
):
    pair = pair_rep.reshape(128, 128)
    upstream = cotangent.reshape(128, 128)
    flat = contact.reshape(256, 16)

    send, proj, gates, scaled_t, mate = call(
        first_kernel,
        [
            ((16, 32, 128), BF),
            ((2, 512, 128), F32),
            ((264, 128), F32),
            ((136, 128), F32),
            ((1,), jnp.int32),
        ],
        my_mate().reshape(1),
        pair,
        norm_gain.reshape(1, 128),
        w_out_proj,
        w_in_proj,
        w_gate,
        update_gain,
        spot=True,
        far=range(1, 7),
    )
    sides = to_channels(send, 1, (0, 2, 3))
    triangles = call(
        forward_kernel,
        ((4, 8, 24, 128), BF),
        mate,
        sides,
        contact,
        flat,
        spot=True,
        far=(2,),
    )
    updated, send, grad_gate = call(
        middle_kernel,
        [((128, 128), BF), ((16, 16, 128), BF), ((256, 128), BF)],
        pair,
        upstream,
        to_pairs(triangles, 1, (0,)),
        gates,
        w_final,
    )
    grads = call(
        backward_kernel,
        ((4, 8, 32, 128), BF),
        mate,
        sides,
        to_channels(send, 1, (0,)),
        contact,
        flat,
        spot=True,
        far=(3,),
    )
    grad_pair = call(
        last_kernel,
        ((128, 128), BF),
        upstream,
        to_pairs(grads, 1, (0, 2, 3)),
        proj,
        grad_gate,
        scaled_t,
        w_out_proj,
        w_in_proj,
        w_gate,
    )
    return (updated.reshape(pair_rep.shape), grad_pair.reshape(pair_rep.shape))


def solution(mesh):
    fine = Mesh(mesh.devices.reshape(4, 4, 4, 4, 2), ("zl", "x", "y", "zh", "core"))
    block = P(("zl", "x"), ("y", "zh", "core"), None)
    in_specs = (block, block, P(), P(), P(), P(), P(), P(), P())
    return jax.shard_map(
        on_device, mesh=fine, in_specs=in_specs, out_specs=(block, block), check_vma=False
    )
```

```python
import functools

import jax
import jax.numpy as jnp
import ml_dtypes
import numpy as np
from jax import lax
from jax.experimental import pallas as pl
from jax.experimental.pallas import tpu as pltpu
from jax.sharding import Mesh
from jax.sharding import PartitionSpec as P


PLANE = ("x", "y", "core")
DEPTH = ("zl", "zh")
EPSILON = 1e-05
BF = jnp.bfloat16
F32 = jnp.float32


def dot(a, b, dims=((1,), (0,))):
    return lax.dot_general(a, b, (dims, ((), ())), preferred_element_type=F32)


def norm(values):
    center = jnp.mean(values, axis=0, keepdims=True)
    shifted = values - center
    inverse = lax.rsqrt(jnp.mean(shifted * shifted, axis=0, keepdims=True) + EPSILON)
    return shifted * inverse, inverse


def norm_back(weighted, scaled, inverse):
    first = jnp.mean(weighted, axis=0, keepdims=True)
    second = jnp.mean(weighted * scaled, axis=0, keepdims=True)
    return inverse * (weighted - first - scaled * second)


def pair_order():
    here = lax.broadcasted_iota(jnp.int32, (128, 128), 0)
    there = lax.broadcasted_iota(jnp.int32, (128, 128), 1)
    same = (here >> 3 == (there & 15)) & ((here & 7) == there >> 4)
    return same.astype(F32).astype(BF)


def column(gain):
    return jnp.broadcast_to(gain, (128, 128)).T


def groups(values):
    return values.reshape(16, 8, 128).astype(BF)


def take(got, array):
    return got[:, 8 * array : 8 * array + 8].astype(F32).reshape(128, 128)


def fetch(pairs, arrived):
    copies = [
        pltpu.make_async_copy(there, here, arrived.at[n]) for n, (there, here) in enumerate(pairs)
    ]
    for copy in copies:
        copy.start()
    return copies


def first_kernel(spot, pair, gain, w_out, w_in, update, send, rest, mate):
    mate[0] = spot[0]
    scaled, inverse = norm(dot(pair[...], pair_order(), ((0,), (0,))))
    normed = (scaled * column(gain[...])).astype(BF)
    rest[0:128] = scaled
    rest[128:129] = inverse
    rest[129:130] = gain[...]
    for half, weights in enumerate((w_out, w_in)):
        p = dot(weights[...], normed, ((0,), (0,)))
        for side in range(2):
            part = 256 * side
            gated = jax.nn.sigmoid(p[part : part + 128]) * p[part + 128 : part + 256]
            row = 16 * half + 8 * side
            send[:, row : row + 8] = groups(gated)
    rest[130:132] = update[...]


def swap_groups(rows):
    rows = list(rows)
    group = lax.broadcasted_iota(jnp.int32, rows[0].shape, 1) >> 4
    step = len(rows) // 2
    while step:
        low = (group & step) == 0
        for a in range(len(rows)):
            if a & step:
                continue
            x, y = rows[a], rows[a + step]
            rows[a] = jnp.where(low, x, pltpu.roll(y, 16 * step, 1))
            rows[a + step] = jnp.where(low, pltpu.roll(x, 128 - 16 * step, 1), y)
        step //= 2
    return rows


def spread_kernel(full, parts, got, send, held_full, held_parts):
    pieces = []
    for high in range(2):
        rows = swap_groups(
            [got[4 * zl + 2 * high + low].astype(F32) for low in range(2) for zl in range(4)]
        )
        for q in range(8):
            held_full[:, 8 * high + q] = rows[q][8 * full : 8 * full + 8]
            pieces.append([rows[q][8 * a : 8 * a + 8] for a in parts])
    if len(parts) == 1:
        pieces = [pieces[q] + pieces[8 + q] for q in range(8)]
    for row, arrays in enumerate(pieces):
        for mate, values in enumerate(swap_groups(arrays + arrays[: 4 - len(arrays)])):
            held_parts[:, mate, row] = values
    values = held_full[...].astype(BF)
    for mate in range(4):
        send[:, mate, 0:16] = values
    send[:, :, 16:] = held_parts[...].astype(BF)


def collect_kernel(full, parts, got, send, held, held_parts, out):
    values = got[...].astype(F32)
    held[...] = values[:, 0, 0:16] + values[:, 1, 0:16] + values[:, 2, 0:16] + values[:, 3, 0:16]
    held_parts[...] = values[:, :, 16:]
    pieces = [
        swap_groups([held_parts[:, mate, row] for mate in range(4)])
        for row in range(got.shape[2] - 16)
    ]
    if len(parts) == 1:
        pieces = [[values[high]] for high in range(2) for values in pieces]
    for high in range(2):
        arrays = {full: [held[:, 8 * high + q] for q in range(8)]}
        for n, a in enumerate(parts):
            arrays[a] = [pieces[8 * high + q][n] for q in range(8)]
        for a, rows in arrays.items():
            for g, values in enumerate(swap_groups(rows)):
                zh = 2 * high + (g >> 2)
                out[4 * (g & 3) + zh, 8 * a : 8 * a + 8] = values
    send[...] = out[...].astype(BF)


def swap_halves(first, second):
    low = lax.broadcasted_iota(jnp.int32, first.shape, 1) < 64
    return (
        jnp.where(low, first, pltpu.roll(second, 64, 1)),
        jnp.where(low, pltpu.roll(first, 64, 1), second),
    )


def whole(got, big):
    tiles = [got[x, :, 0:16].astype(F32).reshape(128, 128) for x in range(4)]
    left = swap_halves(tiles[0], tiles[1])
    right = swap_halves(tiles[2], tiles[3])
    values = jnp.concatenate(
        [jnp.concatenate([left[low], right[low]], axis=1) for low in range(2)], axis=0
    )
    return dot(values.astype(BF), big[0:256])


def quarters(got):
    rows = got.shape[2] - 16
    tiles = [got[x, :, 16:].astype(F32).reshape(8 * rows, 128) for x in range(4)]
    arrays = swap_groups(tiles)
    if rows == 8:
        highs = [values.reshape(8, 1, 8, 128) for values in arrays[:2]]
        arrays = [jnp.concatenate(highs, axis=1).reshape(128, 128)]
    turned = [values.T for values in arrays[:3]]
    return [jnp.concatenate([t[0:64], t[64:128]], axis=1).astype(BF) for t in turned]


def send_whole(send, values, big):
    values = dot(values.astype(BF), big[256:512])
    for half in range(2):
        lanes = slice(128 * half, 128 * half + 128)
        tiles = swap_halves(values[0:128, lanes], values[128:256, lanes])
        for n in range(2):
            send[2 * half + n, :, 0:16] = tiles[n].reshape(8, 16, 128).astype(BF)


def send_quarters(send, arrays):
    rows = [
        jnp.concatenate([values[:, 0:128], values[:, 128:256]], axis=0).T for values in arrays
    ]
    if len(rows) == 1:
        highs = rows[0].reshape(8, 2, 8, 128)
        rows = [highs[:, n].reshape(64, 128) for n in range(2)]
    rows += rows[: 4 - len(rows)]
    for x, tile in enumerate(swap_groups(rows)):
        send[x, :, 16:] = tile.reshape(8, send.shape[2] - 16, 128).astype(BF)


def join(pieces):
    return jnp.concatenate(pieces, axis=0)


NN = ((1,), (0,))
NT = ((1,), (1,))
TN = ((0,), (0,))


def q_block(place):
    return ((place >> 5) & 3) * 4 + ((place >> 3) & 1) * 2 + (place >> 7)


def tables():
    place = np.arange(256)
    residue_p = (((place >> 4) & 3) * 4 + (place >> 6)) * 16 + (place & 15)
    residue_q = q_block(place) * 16 + ((place >> 4) & 1) * 8 + (place & 7)
    order = residue_p[:, None] == residue_q[None, :]
    blocks = q_block(place)[:, None] == place[None, :] >> 4
    long = q_block(place)[:, None] == np.arange(16)[None, :]
    wide = q_block(place)[::8, None] == (place & 15)[None, :]
    big = np.concatenate([order, order.T, blocks], axis=0).astype(ml_dtypes.bfloat16)
    small = np.concatenate([long, long[::8]], axis=0).astype(ml_dtypes.bfloat16)
    return jnp.asarray(big), jnp.asarray(small), jnp.asarray(wide.astype(np.float32))


def masks(contact, flat, mate, big, small, wide):
    by_k = flat[...].astype(F32)
    wanted = lax.broadcasted_iota(jnp.int32, (4, 16), 0) + 4 * mate
    label = lax.broadcasted_iota(jnp.int32, (4, 16), 1)
    by_k = dot((label == wanted).astype(F32).astype(BF), by_k.astype(BF), NT)
    short, long = small[256:288], small[0:256]
    for_out = [
        dot(short, contact[4 * mate + t].astype(F32).astype(BF), NT).astype(BF) for t in range(4)
    ]
    for_in = [(wide[...] * by_k[t : t + 1]).astype(BF) for t in range(4)]
    return dot(join(for_out), long, NT), dot(join(for_in), big[512:768], NT)


def apply(masks, t, values):
    mask = masks[32 * t : 32 * t + 32].reshape(32, 1, 256)
    return (values.reshape(32, 8, 256) * mask).reshape(256, 256)


def forward_kernel(spot, got, contact, flat, big, small, wide, send, made, near, arrived):
    copies = fetch([(contact, near)], arrived)
    left_out, left_in, right_in = quarters(got)
    right_out = whole(got, big)
    copies[0].wait()
    mask_out, mask_in = masks(near, flat, spot[0], big, small, wide)
    made[0:128] = mask_out
    made[128:256] = mask_in
    outs, ins = [], None
    for t in range(4):
        part = slice(16 * t, 16 * t + 16)
        outs.append(dot(left_out[part], apply(mask_out, t, right_out).astype(BF), NN))
        term = apply(mask_in, t, dot(right_in[part], left_in[part], TN))
        ins = term if ins is None else ins + term
    send_whole(send, ins, big)
    send_quarters(send, [join(outs)])


def backward_kernel(got, grads, made, big, send):
    left_out, left_in, right_in = quarters(got)
    grad_out = quarters(grads)[0]
    right_out = whole(got, big)
    grad_in = whole(grads, big)
    mask_out, mask_in = made[0:128], made[128:256]
    grad_left_out, grad_left_in, grad_right_in, grad_right_out = [], [], [], None
    for t in range(4):
        part = slice(16 * t, 16 * t + 16)
        over_j = apply(mask_out, t, right_out).astype(BF)
        grad_left_out.append(dot(grad_out[part], over_j, NT))
        term = apply(mask_out, t, dot(left_out[part], grad_out[part], TN))
        grad_right_out = term if grad_right_out is None else grad_right_out + term
        both = apply(mask_in, t, grad_in).astype(BF)
        grad_left_in.append(dot(right_in[part], both, NN))
        grad_right_in.append(dot(left_in[part], both, NT))
    send_whole(send, grad_right_out, big)
    send_quarters(send, [join(grad_left_out), join(grad_left_in), join(grad_right_in)])


def middle_kernel(pair, cotangent, got, rest, w_gate, w_final, updated, send, grad_gate):
    order = pair_order()
    upstream = dot(cotangent[...], order, TN)
    total = dot(pair[...], order, TN)
    normed_pair = (rest[0:128] * column(rest[129:130])).astype(BF)
    gates = jax.nn.sigmoid(dot(w_gate[...], normed_pair, TN))
    for t in range(2):
        scaled, inverse = norm(take(got, t))
        gain_t = column(rest[130 + t : 131 + t])
        normed = (scaled * gain_t).astype(BF)
        gate = gates[128 * t : 128 * t + 128]
        final = dot(w_final[t], normed, TN)
        total = total + gate * final
        grad_final = (upstream * gate).astype(BF)
        grad_gate[128 * t : 128 * t + 128] = (upstream * final * gate * (1.0 - gate)).astype(BF)
        weighted = dot(w_final[t], grad_final) * gain_t
        send[:, 8 * t : 8 * t + 8] = groups(norm_back(weighted, scaled, inverse))
    updated[...] = dot(order, total.astype(BF), NT).astype(BF)


def last_kernel(cotangent, got, grad_gate, rest, w_out, w_in, w_gate, grad_pair):
    order = pair_order()
    upstream = dot(cotangent[...], order, TN)
    grad_normed = dot(w_gate[...], grad_gate[...])
    scaled, inverse, gain = rest[0:128], rest[128:129], column(rest[129:130])
    normed = (scaled * gain).astype(BF)
    for half, weights in enumerate((w_out, w_in)):
        p = dot(weights[...], normed, TN)
        parts = []
        for side in range(2):
            grad = take(got, 2 * half + side)
            sig = jax.nn.sigmoid(p[256 * side : 256 * side + 128])
            parts.append(grad * p[256 * side + 128 : 256 * side + 256] * sig * (1.0 - sig))
            parts.append(grad * sig)
        grad_normed = grad_normed + dot(
            weights[...], jnp.concatenate(parts, axis=0).astype(BF)
        )
    back = norm_back(grad_normed * gain, scaled, inverse)
    grad_pair[...] = dot(order, (upstream + back).astype(BF), NT).astype(BF)


def call(kernel, out, *args, scratch=(), spot=False, far=(), limit=32 * 1024 * 1024):
    specs = [pl.BlockSpec(memory_space=pltpu.VMEM)] * len(args)
    for n in far:
        specs[n] = pl.BlockSpec(memory_space=pltpu.HBM)
    if spot:
        specs[0] = pl.BlockSpec(memory_space=pltpu.SMEM)
    multi = isinstance(out, list)
    shapes = [jax.ShapeDtypeStruct(s, d) for s, d in (out if multi else [out])]
    outs = [
        pl.BlockSpec(memory_space=pltpu.SMEM if x.dtype == jnp.int32 else pltpu.VMEM)
        for x in shapes
    ]
    buffers = [pltpu.VMEM(args[n].shape, args[n].dtype) for n in far]
    buffers += [pltpu.VMEM(s, F32) for s in scratch]
    if far:
        buffers.append(pltpu.SemaphoreType.DMA((len(far),)))
    params = pltpu.CompilerParams(vmem_limit_bytes=limit) if limit else None
    result = pl.pallas_call(
        kernel,
        out_shape=shapes,
        in_specs=specs,
        out_specs=outs,
        scratch_shapes=buffers,
        compiler_params=params,
    )(*args)
    return result if multi else result[0]


def exchange(values, axis):
    return lax.all_to_all(values, axis, 0, 0, tiled=True)


def to_channels(send, full, parts):
    rows = 24 if len(parts) == 1 else 32
    spread = call(
        functools.partial(spread_kernel, full, parts),
        ((8, 4, rows, 128), BF),
        exchange(send, DEPTH),
        scratch=[(8, 16, 128), (8, 4, rows - 16, 128)],
    )
    return exchange(spread.reshape(32, rows, 128), PLANE).reshape(4, 8, rows, 128)


def to_pairs(send, full, parts):
    rows = send.shape[2]
    amount = 8 + 8 * len(parts)
    back = call(
        functools.partial(collect_kernel, full, parts),
        ((16, amount, 128), BF),
        exchange(send.reshape(32, rows, 128), PLANE).reshape(8, 4, rows, 128),
        scratch=[(8, 16, 128), (8, 4, rows - 16, 128), (16, amount, 128)],
    )
    return exchange(back, DEPTH)


def my_mate():
    return lax.axis_index(PLANE) & 3


def on_device(
    pair_rep, cotangent, contact, norm_gain, w_out_proj, w_in_proj, update_gain, w_gate, w_final
):
    pair = pair_rep.reshape(128, 128)
    upstream = cotangent.reshape(128, 128)
    flat = contact.reshape(256, 16)

    send, rest, mate = call(
        first_kernel,
        [((16, 32, 128), BF), ((136, 128), F32), ((1,), jnp.int32)],
        my_mate().reshape(1),
        pair,
        norm_gain.reshape(1, 128),
        w_out_proj,
        w_in_proj,
        update_gain,
        spot=True,
        limit=None,
    )
    sides = to_channels(send, 1, (0, 2, 3))
    big, small, wide = tables()
    triangles, made = call(
        forward_kernel,
        [((4, 8, 24, 128), BF), ((256, 256), F32)],
        mate,
        sides,
        contact,
        flat,
        big,
        small,
        wide,
        spot=True,
        far=(2,),
    )
    updated, send, grad_gate = call(
        middle_kernel,
        [((128, 128), BF), ((16, 16, 128), BF), ((256, 128), BF)],
        pair,
        upstream,
        to_pairs(triangles, 1, (0,)),
        rest,
        w_gate,
        w_final,
    )
    grads = call(
        backward_kernel,
        ((4, 8, 32, 128), BF),
        sides,
        to_channels(send, 1, (0,)),
        made,
        big,
    )
    grad_pair = call(
        last_kernel,
        ((128, 128), BF),
        upstream,
        to_pairs(grads, 1, (0, 2, 3)),
        grad_gate,
        rest,
        w_out_proj,
        w_in_proj,
        w_gate,
    )
    return (updated.reshape(pair_rep.shape), grad_pair.reshape(pair_rep.shape))


def solution(mesh):
    fine = Mesh(mesh.devices.reshape(4, 4, 4, 4, 2), ("zl", "x", "y", "zh", "core"))
    block = P(("zl", "x"), ("y", "zh", "core"), None)
    in_specs = (block, block, P(), P(), P(), P(), P(), P(), P())
    return jax.shard_map(
        on_device, mesh=fine, in_specs=in_specs, out_specs=(block, block), check_vma=False
    )
```

```python
import functools

import jax
import jax.numpy as jnp
import ml_dtypes
import numpy as np
from jax import lax
from jax.experimental import pallas as pl
from jax.experimental.pallas import tpu as pltpu
from jax.sharding import Mesh
from jax.sharding import PartitionSpec as P


PLANE = ("x", "y", "core")
DEPTH = ("zl", "zh")
EPSILON = 1e-05
BF = jnp.bfloat16
F32 = jnp.float32


def dot(a, b, dims=((1,), (0,))):
    return lax.dot_general(a, b, (dims, ((), ())), preferred_element_type=F32)


def norm(values):
    center = jnp.mean(values, axis=0, keepdims=True)
    shifted = values - center
    inverse = lax.rsqrt(jnp.mean(shifted * shifted, axis=0, keepdims=True) + EPSILON)
    return shifted * inverse, inverse


def norm_back(weighted, scaled, inverse):
    first = jnp.mean(weighted, axis=0, keepdims=True)
    second = jnp.mean(weighted * scaled, axis=0, keepdims=True)
    return inverse * (weighted - first - scaled * second)


def pair_order():
    here = lax.broadcasted_iota(jnp.int32, (128, 128), 0)
    there = lax.broadcasted_iota(jnp.int32, (128, 128), 1)
    same = (here >> 3 == (there & 15)) & ((here & 7) == there >> 4)
    return same.astype(F32).astype(BF)


def column(gain):
    return jnp.broadcast_to(gain, (128, 128)).T


def groups(values):
    return values.reshape(16, 8, 128).astype(BF)


def take(got, array):
    return got[:, 8 * array : 8 * array + 8].astype(F32).reshape(128, 128)


def swap_groups(rows):
    rows = list(rows)
    group = lax.broadcasted_iota(jnp.int32, rows[0].shape, 1) >> 4
    step = len(rows) // 2
    while step:
        low = (group & step) == 0
        for a in range(len(rows)):
            if a & step:
                continue
            x, y = rows[a], rows[a + step]
            rows[a] = jnp.where(low, x, pltpu.roll(y, 16 * step, 1))
            rows[a + step] = jnp.where(low, pltpu.roll(x, 128 - 16 * step, 1), y)
        step //= 2
    return rows


def spread_kernel(full, parts, got, send, held_full, held_parts):
    pieces = []
    for high in range(2):
        rows = swap_groups(
            [got[4 * zl + 2 * high + low].astype(F32) for low in range(2) for zl in range(4)]
        )
        for q in range(8):
            held_full[:, 8 * high + q] = rows[q][8 * full : 8 * full + 8]
            pieces.append([rows[q][8 * a : 8 * a + 8] for a in parts])
    if len(parts) == 1:
        pieces = [pieces[q] + pieces[8 + q] for q in range(8)]
    for row, arrays in enumerate(pieces):
        for mate, values in enumerate(swap_groups(arrays + arrays[: 4 - len(arrays)])):
            held_parts[:, mate, row] = values
    values = held_full[...].astype(BF)
    for mate in range(4):
        send[:, mate, 0:16] = values
    send[:, :, 16:] = held_parts[...].astype(BF)


def collect_kernel(full, parts, got, send, held, held_parts, out):
    values = got[...].astype(F32)
    held[...] = values[:, 0, 0:16] + values[:, 1, 0:16] + values[:, 2, 0:16] + values[:, 3, 0:16]
    held_parts[...] = values[:, :, 16:]
    pieces = [
        swap_groups([held_parts[:, mate, row] for mate in range(4)])
        for row in range(got.shape[2] - 16)
    ]
    if len(parts) == 1:
        pieces = [[values[high]] for high in range(2) for values in pieces]
    for high in range(2):
        arrays = {full: [held[:, 8 * high + q] for q in range(8)]}
        for n, a in enumerate(parts):
            arrays[a] = [pieces[8 * high + q][n] for q in range(8)]
        for a, rows in arrays.items():
            for g, values in enumerate(swap_groups(rows)):
                zh = 2 * high + (g >> 2)
                out[4 * (g & 3) + zh, 8 * a : 8 * a + 8] = values
    send[...] = out[...].astype(BF)


def swap_halves(first, second):
    low = lax.broadcasted_iota(jnp.int32, first.shape, 1) < 64
    return (
        jnp.where(low, first, pltpu.roll(second, 64, 1)),
        jnp.where(low, pltpu.roll(first, 64, 1), second),
    )


def whole(got, big):
    tiles = [got[x, :, 0:16].astype(F32).reshape(128, 128) for x in range(4)]
    left = swap_halves(tiles[0], tiles[1])
    right = swap_halves(tiles[2], tiles[3])
    values = jnp.concatenate(
        [jnp.concatenate([left[low], right[low]], axis=1) for low in range(2)], axis=0
    )
    return dot(values.astype(BF), big[0:256])


def quarters(got):
    rows = got.shape[2] - 16
    tiles = [got[x, :, 16:].astype(F32).reshape(8 * rows, 128) for x in range(4)]
    arrays = swap_groups(tiles)
    if rows == 8:
        highs = [values.reshape(8, 1, 8, 128) for values in arrays[:2]]
        arrays = [jnp.concatenate(highs, axis=1).reshape(128, 128)]
    turned = [values.T for values in arrays[:3]]
    return [jnp.concatenate([t[0:64], t[64:128]], axis=1).astype(BF) for t in turned]


def send_whole(send, values, big):
    values = dot(values.astype(BF), big[256:512])
    for half in range(2):
        lanes = slice(128 * half, 128 * half + 128)
        tiles = swap_halves(values[0:128, lanes], values[128:256, lanes])
        for n in range(2):
            send[2 * half + n, :, 0:16] = tiles[n].reshape(8, 16, 128).astype(BF)


def send_quarters(send, arrays):
    rows = [
        jnp.concatenate([values[:, 0:128], values[:, 128:256]], axis=0).T for values in arrays
    ]
    if len(rows) == 1:
        highs = rows[0].reshape(8, 2, 8, 128)
        rows = [highs[:, n].reshape(64, 128) for n in range(2)]
    rows += rows[: 4 - len(rows)]
    for x, tile in enumerate(swap_groups(rows)):
        send[x, :, 16:] = tile.reshape(8, send.shape[2] - 16, 128).astype(BF)


def join(pieces):
    return jnp.concatenate(pieces, axis=0)


NN = ((1,), (0,))
NT = ((1,), (1,))
TN = ((0,), (0,))


def q_block(place):
    return ((place >> 5) & 3) * 4 + ((place >> 3) & 1) * 2 + (place >> 7)


def tables():
    place = np.arange(256)
    residue_p = (((place >> 4) & 3) * 4 + (place >> 6)) * 16 + (place & 15)
    residue_q = q_block(place) * 16 + ((place >> 4) & 1) * 8 + (place & 7)
    order = residue_p[:, None] == residue_q[None, :]
    blocks = q_block(place)[:, None] == place[None, :] >> 4
    long = q_block(place)[:, None] == np.arange(16)[None, :]
    wide = q_block(place)[::8, None] == (place & 15)[None, :]
    big = np.concatenate([order, order.T], axis=0)
    small = np.concatenate([long, long[::8]], axis=0)
    big, blocks, small = (jnp.asarray(x.astype(ml_dtypes.bfloat16)) for x in (big, blocks, small))
    return big, blocks, small, jnp.asarray(wide.astype(np.float32))


def masks(contact, flat, mate, blocks, small, wide):
    by_k = flat[...].astype(F32)
    wanted = lax.broadcasted_iota(jnp.int32, (4, 16), 0) + 4 * mate
    label = lax.broadcasted_iota(jnp.int32, (4, 16), 1)
    by_k = dot((label == wanted).astype(F32).astype(BF), by_k.astype(BF), NT)
    short, long = small[256:288], small[0:256]
    for_out = [
        dot(short, contact[4 * mate + t].astype(F32).astype(BF), NT).astype(BF) for t in range(4)
    ]
    for_in = [(wide[...] * by_k[t : t + 1]).astype(BF) for t in range(4)]
    return dot(join(for_out), long, NT), dot(join(for_in), blocks[...], NT)


def apply(masks, t, values):
    mask = masks[32 * t : 32 * t + 32].reshape(32, 1, 256)
    return (values.reshape(32, 8, 256) * mask).reshape(256, 256)


def forward_kernel(got, made, big, send):
    left_out, left_in, right_in = quarters(got)
    right_out = whole(got, big)
    mask_out, mask_in = made[0:128], made[128:256]
    outs, ins = [], None
    for t in range(4):
        part = slice(16 * t, 16 * t + 16)
        outs.append(dot(left_out[part], apply(mask_out, t, right_out).astype(BF), NN))
        term = apply(mask_in, t, dot(right_in[part], left_in[part], TN))
        ins = term if ins is None else ins + term
    send_whole(send, ins, big)
    send_quarters(send, [join(outs)])


def backward_kernel(got, grads, made, big, send):
    left_out, left_in, right_in = quarters(got)
    grad_out = quarters(grads)[0]
    right_out = whole(got, big)
    grad_in = whole(grads, big)
    mask_out, mask_in = made[0:128], made[128:256]
    grad_left_out, grad_left_in, grad_right_in, grad_right_out = [], [], [], None
    for t in range(4):
        part = slice(16 * t, 16 * t + 16)
        over_j = apply(mask_out, t, right_out).astype(BF)
        grad_left_out.append(dot(grad_out[part], over_j, NT))
        term = apply(mask_out, t, dot(left_out[part], grad_out[part], TN))
        grad_right_out = term if grad_right_out is None else grad_right_out + term
        both = apply(mask_in, t, grad_in).astype(BF)
        grad_left_in.append(dot(right_in[part], both, NN))
        grad_right_in.append(dot(left_in[part], both, NT))
    send_whole(send, grad_right_out, big)
    send_quarters(send, [join(grad_left_out), join(grad_left_in), join(grad_right_in)])


def first_kernel(
    spot, pair, gain, w_out, w_in, update, contact, flat, blocks, small, wide, send, rest, made, proj
):
    scaled, inverse = norm(dot(pair[...], pair_order(), ((0,), (0,))))
    normed = (scaled * column(gain[...])).astype(BF)
    rest[0:128] = scaled
    rest[128:129] = inverse
    rest[129:130] = gain[...]
    for half, weights in enumerate((w_out, w_in)):
        p = dot(weights[...], normed, ((0,), (0,)))
        proj[half] = p
        for side in range(2):
            part = 256 * side
            gated = jax.nn.sigmoid(p[part : part + 128]) * p[part + 128 : part + 256]
            row = 16 * half + 8 * side
            send[:, row : row + 8] = groups(gated)
    rest[130:132] = update[...]
    mask_out, mask_in = masks(contact, flat, spot[0], blocks, small, wide)
    made[0:128] = mask_out
    made[128:256] = mask_in


def middle_kernel(pair, cotangent, got, rest, w_gate, w_final, updated, send, grad_gate):
    order = pair_order()
    upstream = dot(cotangent[...], order, TN)
    total = dot(pair[...], order, TN)
    normed_pair = (rest[0:128] * column(rest[129:130])).astype(BF)
    gates = jax.nn.sigmoid(dot(w_gate[...], normed_pair, TN))
    for t in range(2):
        scaled, inverse = norm(take(got, t))
        gain_t = column(rest[130 + t : 131 + t])
        normed = (scaled * gain_t).astype(BF)
        gate = gates[128 * t : 128 * t + 128]
        final = dot(w_final[t], normed, TN)
        total = total + gate * final
        grad_final = (upstream * gate).astype(BF)
        grad_gate[128 * t : 128 * t + 128] = (upstream * final * gate * (1.0 - gate)).astype(BF)
        weighted = dot(w_final[t], grad_final) * gain_t
        send[:, 8 * t : 8 * t + 8] = groups(norm_back(weighted, scaled, inverse))
    updated[...] = dot(order, total.astype(BF), NT).astype(BF)


def last_kernel(cotangent, got, grad_gate, rest, proj, w_out, w_in, w_gate, grad_pair):
    order = pair_order()
    upstream = dot(cotangent[...], order, TN)
    grad_normed = dot(w_gate[...], grad_gate[...])
    scaled, inverse, gain = rest[0:128], rest[128:129], column(rest[129:130])
    for half, weights in enumerate((w_out, w_in)):
        p = proj[half]
        parts = []
        for side in range(2):
            grad = take(got, 2 * half + side)
            sig = jax.nn.sigmoid(p[256 * side : 256 * side + 128])
            parts.append(grad * p[256 * side + 128 : 256 * side + 256] * sig * (1.0 - sig))
            parts.append(grad * sig)
        grad_normed = grad_normed + dot(
            weights[...], jnp.concatenate(parts, axis=0).astype(BF)
        )
    back = norm_back(grad_normed * gain, scaled, inverse)
    grad_pair[...] = dot(order, (upstream + back).astype(BF), NT).astype(BF)


def call(kernel, out, *args, scratch=(), spot=False, limit=32 * 1024 * 1024):
    specs = [pl.BlockSpec(memory_space=pltpu.VMEM)] * len(args)
    if spot:
        specs[0] = pl.BlockSpec(memory_space=pltpu.SMEM)
    multi = isinstance(out, list)
    shapes = [jax.ShapeDtypeStruct(s, d) for s, d in (out if multi else [out])]
    outs = [pl.BlockSpec(memory_space=pltpu.VMEM)] * len(shapes)
    params = pltpu.CompilerParams(vmem_limit_bytes=limit) if limit else None
    result = pl.pallas_call(
        kernel,
        out_shape=shapes,
        in_specs=specs,
        out_specs=outs,
        scratch_shapes=[pltpu.VMEM(s, F32) for s in scratch],
        compiler_params=params,
    )(*args)
    return result if multi else result[0]


def exchange(values, axis):
    return lax.all_to_all(values, axis, 0, 0, tiled=True)


def to_channels(send, full, parts):
    rows = 24 if len(parts) == 1 else 32
    spread = call(
        functools.partial(spread_kernel, full, parts),
        ((8, 4, rows, 128), BF),
        exchange(send, DEPTH),
        scratch=[(8, 16, 128), (8, 4, rows - 16, 128)],
    )
    return exchange(spread.reshape(32, rows, 128), PLANE).reshape(4, 8, rows, 128)


def to_pairs(send, full, parts):
    rows = send.shape[2]
    amount = 8 + 8 * len(parts)
    back = call(
        functools.partial(collect_kernel, full, parts),
        ((16, amount, 128), BF),
        exchange(send.reshape(32, rows, 128), PLANE).reshape(8, 4, rows, 128),
        scratch=[(8, 16, 128), (8, 4, rows - 16, 128), (16, amount, 128)],
    )
    return exchange(back, DEPTH)


def my_mate():
    return lax.axis_index(PLANE) & 3


def on_device(
    pair_rep, cotangent, contact, norm_gain, w_out_proj, w_in_proj, update_gain, w_gate, w_final
):
    pair = pair_rep.reshape(128, 128)
    upstream = cotangent.reshape(128, 128)
    flat = contact.reshape(256, 16)

    big, blocks, small, wide = tables()
    send, rest, made, proj = call(
        first_kernel,
        [
            ((16, 32, 128), BF),
            ((136, 128), F32),
            ((256, 256), F32),
            ((2, 512, 128), F32),
        ],
        my_mate().reshape(1),
        pair,
        norm_gain.reshape(1, 128),
        w_out_proj,
        w_in_proj,
        update_gain,
        contact,
        flat,
        blocks,
        small,
        wide,
        spot=True,
        limit=None,
    )
    sides = to_channels(send, 1, (0, 2, 3))
    triangles = call(forward_kernel, ((4, 8, 24, 128), BF), sides, made, big)
    updated, send, grad_gate = call(
        middle_kernel,
        [((128, 128), BF), ((16, 16, 128), BF), ((256, 128), BF)],
        pair,
        upstream,
        to_pairs(triangles, 1, (0,)),
        rest,
        w_gate,
        w_final,
    )
    grads = call(
        backward_kernel,
        ((4, 8, 32, 128), BF),
        sides,
        to_channels(send, 1, (0,)),
        made,
        big,
    )
    grad_pair = call(
        last_kernel,
        ((128, 128), BF),
        upstream,
        to_pairs(grads, 1, (0, 2, 3)),
        grad_gate,
        rest,
        proj,
        w_out_proj,
        w_in_proj,
        w_gate,
    )
    return (updated.reshape(pair_rep.shape), grad_pair.reshape(pair_rep.shape))


def solution(mesh):
    fine = Mesh(mesh.devices.reshape(4, 4, 4, 4, 2), ("zl", "x", "y", "zh", "core"))
    block = P(("zl", "x"), ("y", "zh", "core"), None)
    in_specs = (block, block, P(), P(), P(), P(), P(), P(), P())
    return jax.shard_map(
        on_device, mesh=fine, in_specs=in_specs, out_specs=(block, block), check_vma=False
    )
```

```python
import functools

import jax
import jax.numpy as jnp
import ml_dtypes
import numpy as np
from jax import lax
from jax.experimental import pallas as pl
from jax.experimental.pallas import tpu as pltpu
from jax.sharding import Mesh
from jax.sharding import PartitionSpec as P


PLANE = ("x", "y", "core")
DEPTH = ("zl", "zh")
EPSILON = 1e-05
BF = jnp.bfloat16
F32 = jnp.float32


def dot(a, b, dims=((1,), (0,))):
    return lax.dot_general(a, b, (dims, ((), ())), preferred_element_type=F32)


def norm(values):
    center = jnp.mean(values, axis=0, keepdims=True)
    shifted = values - center
    inverse = lax.rsqrt(jnp.mean(shifted * shifted, axis=0, keepdims=True) + EPSILON)
    return shifted * inverse, inverse


def norm_back(weighted, scaled, inverse):
    first = jnp.mean(weighted, axis=0, keepdims=True)
    second = jnp.mean(weighted * scaled, axis=0, keepdims=True)
    return inverse * (weighted - first - scaled * second)


def pair_order():
    here = lax.broadcasted_iota(jnp.int32, (128, 128), 0)
    there = lax.broadcasted_iota(jnp.int32, (128, 128), 1)
    same = (here >> 3 == (there & 15)) & ((here & 7) == there >> 4)
    return same.astype(F32).astype(BF)


def column(gain):
    return jnp.broadcast_to(gain, (128, 128)).T


def groups(values):
    return values.reshape(16, 8, 128).astype(BF)


def take(got, array):
    return got[:, 8 * array : 8 * array + 8].astype(F32).reshape(128, 128)


def swap_groups(rows):
    rows = list(rows)
    group = lax.broadcasted_iota(jnp.int32, rows[0].shape, 1) >> 4
    step = len(rows) // 2
    while step:
        low = (group & step) == 0
        for a in range(len(rows)):
            if a & step:
                continue
            x, y = rows[a], rows[a + step]
            rows[a] = jnp.where(low, x, pltpu.roll(y, 16 * step, 1))
            rows[a + step] = jnp.where(low, pltpu.roll(x, 128 - 16 * step, 1), y)
        step //= 2
    return rows


def spread_kernel(full, parts, got, send, held_full, held_parts):
    pieces = []
    for high in range(2):
        rows = swap_groups(
            [got[4 * zl + 2 * high + low].astype(F32) for low in range(2) for zl in range(4)]
        )
        for q in range(8):
            held_full[:, 8 * high + q] = rows[q][8 * full : 8 * full + 8]
            pieces.append([rows[q][8 * a : 8 * a + 8] for a in parts])
    if len(parts) == 1:
        pieces = [pieces[q] + pieces[8 + q] for q in range(8)]
    for row, arrays in enumerate(pieces):
        for mate, values in enumerate(swap_groups(arrays + arrays[: 4 - len(arrays)])):
            held_parts[:, mate, row] = values
    values = held_full[...].astype(BF)
    for mate in range(4):
        send[:, mate, 0:16] = values
    send[:, :, 16:] = held_parts[...].astype(BF)


def collect_kernel(full, parts, got, send, held, held_parts, out):
    values = got[...].astype(F32)
    held[...] = values[:, 0, 0:16] + values[:, 1, 0:16] + values[:, 2, 0:16] + values[:, 3, 0:16]
    held_parts[...] = values[:, :, 16:]
    pieces = [
        swap_groups([held_parts[:, mate, row] for mate in range(4)])
        for row in range(got.shape[2] - 16)
    ]
    if len(parts) == 1:
        pieces = [[values[high]] for high in range(2) for values in pieces]
    for high in range(2):
        arrays = {full: [held[:, 8 * high + q] for q in range(8)]}
        for n, a in enumerate(parts):
            arrays[a] = [pieces[8 * high + q][n] for q in range(8)]
        for a, rows in arrays.items():
            for g, values in enumerate(swap_groups(rows)):
                zh = 2 * high + (g >> 2)
                out[4 * (g & 3) + zh, 8 * a : 8 * a + 8] = values
    send[...] = out[...].astype(BF)


def swap_halves(first, second):
    low = lax.broadcasted_iota(jnp.int32, first.shape, 1) < 64
    return (
        jnp.where(low, first, pltpu.roll(second, 64, 1)),
        jnp.where(low, pltpu.roll(first, 64, 1), second),
    )


def whole(got, big):
    tiles = [got[x, :, 0:16].astype(F32).reshape(128, 128) for x in range(4)]
    left = swap_halves(tiles[0], tiles[1])
    right = swap_halves(tiles[2], tiles[3])
    values = jnp.concatenate(
        [jnp.concatenate([left[low], right[low]], axis=1) for low in range(2)], axis=0
    )
    return dot(values.astype(BF), big[0:256])


def quarters(got):
    rows = got.shape[2] - 16
    tiles = [got[x, :, 16:].astype(F32).reshape(8 * rows, 128) for x in range(4)]
    arrays = swap_groups(tiles)
    if rows == 8:
        highs = [values.reshape(8, 1, 8, 128) for values in arrays[:2]]
        arrays = [jnp.concatenate(highs, axis=1).reshape(128, 128)]
    turned = [values.T for values in arrays[:3]]
    return [jnp.concatenate([t[0:64], t[64:128]], axis=1).astype(BF) for t in turned]


def send_whole(send, values, big):
    values = dot(values.astype(BF), big[256:512])
    for half in range(2):
        lanes = slice(128 * half, 128 * half + 128)
        tiles = swap_halves(values[0:128, lanes], values[128:256, lanes])
        for n in range(2):
            send[2 * half + n, :, 0:16] = tiles[n].reshape(8, 16, 128).astype(BF)


def send_quarters(send, arrays):
    rows = [
        jnp.concatenate([values[:, 0:128], values[:, 128:256]], axis=0).T for values in arrays
    ]
    if len(rows) == 1:
        highs = rows[0].reshape(8, 2, 8, 128)
        rows = [highs[:, n].reshape(64, 128) for n in range(2)]
    rows += rows[: 4 - len(rows)]
    for x, tile in enumerate(swap_groups(rows)):
        send[x, :, 16:] = tile.reshape(8, send.shape[2] - 16, 128).astype(BF)


def join(pieces):
    return jnp.concatenate(pieces, axis=0)


NN = ((1,), (0,))
NT = ((1,), (1,))
TN = ((0,), (0,))


def q_block(place):
    return ((place >> 5) & 3) * 4 + ((place >> 3) & 1) * 2 + (place >> 7)


def tables():
    place = np.arange(256)
    residue_p = (((place >> 4) & 3) * 4 + (place >> 6)) * 16 + (place & 15)
    residue_q = q_block(place) * 16 + ((place >> 4) & 1) * 8 + (place & 7)
    order = residue_p[:, None] == residue_q[None, :]
    blocks = q_block(place)[:, None] == place[None, :] >> 4
    long = q_block(place)[:, None] == np.arange(16)[None, :]
    wide = q_block(place)[::8, None] == (place & 15)[None, :]
    big = np.concatenate([order, order.T], axis=0)
    small = np.concatenate([long, long[::8]], axis=0)
    big, blocks, small = (jnp.asarray(x.astype(ml_dtypes.bfloat16)) for x in (big, blocks, small))
    return big, blocks, small, jnp.asarray(wide.astype(np.float32))


def masks(contact, flat, mate, blocks, small, wide):
    by_k = flat[...].astype(F32)
    wanted = lax.broadcasted_iota(jnp.int32, (4, 16), 0) + 4 * mate
    label = lax.broadcasted_iota(jnp.int32, (4, 16), 1)
    by_k = dot((label == wanted).astype(F32).astype(BF), by_k.astype(BF), NT)
    short, long = small[256:288], small[0:256]
    for_out = [
        dot(short, contact[4 * mate + t].astype(F32).astype(BF), NT).astype(BF) for t in range(4)
    ]
    for_in = [(wide[...] * by_k[t : t + 1]).astype(BF) for t in range(4)]
    return dot(join(for_out), long, NT), dot(join(for_in), blocks[...], NT)


def apply(masks, t, values):
    mask = masks[32 * t : 32 * t + 32].reshape(32, 1, 256)
    return (values.reshape(32, 8, 256) * mask).reshape(256, 256)


def forward_kernel(got, made, big, send):
    left_out, left_in, right_in = quarters(got)
    right_out = whole(got, big)
    mask_out, mask_in = made[0:128], made[128:256]
    outs, ins = [], None
    for t in range(4):
        part = slice(16 * t, 16 * t + 16)
        outs.append(dot(left_out[part], apply(mask_out, t, right_out).astype(BF), NN))
        term = apply(mask_in, t, dot(right_in[part], left_in[part], TN))
        ins = term if ins is None else ins + term
    send_whole(send, ins, big)
    send_quarters(send, [join(outs)])


def backward_kernel(got, grads, made, big, send):
    left_out, left_in, right_in = quarters(got)
    grad_out = quarters(grads)[0]
    right_out = whole(got, big)
    grad_in = whole(grads, big)
    mask_out, mask_in = made[0:128], made[128:256]
    grad_left_out, grad_left_in, grad_right_in, grad_right_out = [], [], [], None
    for t in range(4):
        part = slice(16 * t, 16 * t + 16)
        over_j = apply(mask_out, t, right_out).astype(BF)
        grad_left_out.append(dot(grad_out[part], over_j, NT))
        term = apply(mask_out, t, dot(left_out[part], grad_out[part], TN))
        grad_right_out = term if grad_right_out is None else grad_right_out + term
        both = apply(mask_in, t, grad_in).astype(BF)
        grad_left_in.append(dot(right_in[part], both, NN))
        grad_right_in.append(dot(left_in[part], both, NT))
    send_whole(send, grad_right_out, big)
    send_quarters(send, [join(grad_left_out), join(grad_left_in), join(grad_right_in)])


def first_kernel(
    spot, pair, gain, w_out, w_in, update, contact, flat, blocks, small, wide, send, rest, made, proj
):
    scaled, inverse = norm(dot(pair[...], pair_order(), ((0,), (0,))))
    normed = (scaled * column(gain[...])).astype(BF)
    rest[0:128] = scaled
    rest[128:129] = inverse
    rest[129:130] = gain[...]
    for half, weights in enumerate((w_out, w_in)):
        p = dot(weights[...], normed, ((0,), (0,)))
        proj[half] = p
        for side in range(2):
            part = 256 * side
            gated = jax.nn.sigmoid(p[part : part + 128]) * p[part + 128 : part + 256]
            row = 16 * half + 8 * side
            send[:, row : row + 8] = groups(gated)
    rest[130:132] = update[...]
    mask_out, mask_in = masks(contact, flat, spot[0], blocks, small, wide)
    made[0:128] = mask_out
    made[128:256] = mask_in


def middle_kernel(pair, cotangent, got, rest, w_gate, w_final, final, send, grad_gate):
    order = pair_order()
    upstream = dot(cotangent[...], order, TN)
    total = dot(pair[...], order, TN)
    normed_pair = (rest[0:128] * column(rest[129:130])).astype(BF)
    gates = jax.nn.sigmoid(dot(w_gate[...], normed_pair, TN))
    for t in range(2):
        scaled, inverse = norm(take(got, t))
        gain_t = column(rest[130 + t : 131 + t])
        normed = (scaled * gain_t).astype(BF)
        gate = gates[128 * t : 128 * t + 128]
        product = dot(w_final[t], normed, TN)
        total = total + gate * product
        grad_final = (upstream * gate).astype(BF)
        grad_gate[128 * t : 128 * t + 128] = (upstream * product * gate * (1.0 - gate)).astype(BF)
        weighted = dot(w_final[t], grad_final) * gain_t
        send[:, 8 * t : 8 * t + 8] = groups(norm_back(weighted, scaled, inverse))
    final[...] = total.astype(BF)


def last_kernel(
    cotangent, got, grad_gate, rest, proj, final, w_out, w_in, w_gate, updated, grad_pair
):
    order = pair_order()
    upstream = dot(cotangent[...], order, TN)
    updated[...] = dot(order, final[...], NT).astype(BF)
    grad_normed = dot(w_gate[...], grad_gate[...])
    scaled, inverse, gain = rest[0:128], rest[128:129], column(rest[129:130])
    for half, weights in enumerate((w_out, w_in)):
        p = proj[half]
        parts = []
        for side in range(2):
            grad = take(got, 2 * half + side)
            sig = jax.nn.sigmoid(p[256 * side : 256 * side + 128])
            parts.append(grad * p[256 * side + 128 : 256 * side + 256] * sig * (1.0 - sig))
            parts.append(grad * sig)
        grad_normed = grad_normed + dot(
            weights[...], jnp.concatenate(parts, axis=0).astype(BF)
        )
    back = norm_back(grad_normed * gain, scaled, inverse)
    grad_pair[...] = dot(order, (upstream + back).astype(BF), NT).astype(BF)


def call(kernel, out, *args, scratch=(), spot=False, limit=32 * 1024 * 1024):
    specs = [pl.BlockSpec(memory_space=pltpu.VMEM)] * len(args)
    if spot:
        specs[0] = pl.BlockSpec(memory_space=pltpu.SMEM)
    multi = isinstance(out, list)
    shapes = [jax.ShapeDtypeStruct(s, d) for s, d in (out if multi else [out])]
    outs = [pl.BlockSpec(memory_space=pltpu.VMEM)] * len(shapes)
    params = pltpu.CompilerParams(vmem_limit_bytes=limit) if limit else None
    result = pl.pallas_call(
        kernel,
        out_shape=shapes,
        in_specs=specs,
        out_specs=outs,
        scratch_shapes=[pltpu.VMEM(s, F32) for s in scratch],
        compiler_params=params,
    )(*args)
    return result if multi else result[0]


def exchange(values, axis):
    return lax.all_to_all(values, axis, 0, 0, tiled=True)


def to_channels(send, full, parts):
    rows = 24 if len(parts) == 1 else 32
    spread = call(
        functools.partial(spread_kernel, full, parts),
        ((8, 4, rows, 128), BF),
        exchange(send, DEPTH),
        scratch=[(8, 16, 128), (8, 4, rows - 16, 128)],
    )
    return exchange(spread.reshape(32, rows, 128), PLANE).reshape(4, 8, rows, 128)


def to_pairs(send, full, parts):
    rows = send.shape[2]
    amount = 8 + 8 * len(parts)
    back = call(
        functools.partial(collect_kernel, full, parts),
        ((16, amount, 128), BF),
        exchange(send.reshape(32, rows, 128), PLANE).reshape(8, 4, rows, 128),
        scratch=[(8, 16, 128), (8, 4, rows - 16, 128), (16, amount, 128)],
    )
    return exchange(back, DEPTH)


def my_mate():
    return lax.axis_index(PLANE) & 3


def on_device(
    pair_rep, cotangent, contact, norm_gain, w_out_proj, w_in_proj, update_gain, w_gate, w_final
):
    pair = pair_rep.reshape(128, 128)
    upstream = cotangent.reshape(128, 128)
    flat = contact.reshape(256, 16)

    big, blocks, small, wide = tables()
    send, rest, made, proj = call(
        first_kernel,
        [
            ((16, 32, 128), BF),
            ((136, 128), F32),
            ((256, 256), F32),
            ((2, 512, 128), F32),
        ],
        my_mate().reshape(1),
        pair,
        norm_gain.reshape(1, 128),
        w_out_proj,
        w_in_proj,
        update_gain,
        contact,
        flat,
        blocks,
        small,
        wide,
        spot=True,
        limit=None,
    )
    sides = to_channels(send, 1, (0, 2, 3))
    triangles = call(forward_kernel, ((4, 8, 24, 128), BF), sides, made, big)
    final, send, grad_gate = call(
        middle_kernel,
        [((128, 128), BF), ((16, 16, 128), BF), ((256, 128), BF)],
        pair,
        upstream,
        to_pairs(triangles, 1, (0,)),
        rest,
        w_gate,
        w_final,
    )
    grads = call(
        backward_kernel,
        ((4, 8, 32, 128), BF),
        sides,
        to_channels(send, 1, (0,)),
        made,
        big,
    )
    updated, grad_pair = call(
        last_kernel,
        [((128, 128), BF), ((128, 128), BF)],
        upstream,
        to_pairs(grads, 1, (0, 2, 3)),
        grad_gate,
        rest,
        proj,
        final,
        w_out_proj,
        w_in_proj,
        w_gate,
    )
    return (updated.reshape(pair_rep.shape), grad_pair.reshape(pair_rep.shape))


def solution(mesh):
    fine = Mesh(mesh.devices.reshape(4, 4, 4, 4, 2), ("zl", "x", "y", "zh", "core"))
    block = P(("zl", "x"), ("y", "zh", "core"), None)
    in_specs = (block, block, P(), P(), P(), P(), P(), P(), P())
    return jax.shard_map(
        on_device, mesh=fine, in_specs=in_specs, out_specs=(block, block), check_vma=False
    )
```

```python
import functools

import jax
import jax.numpy as jnp
import ml_dtypes
import numpy as np
from jax import lax
from jax.experimental import pallas as pl
from jax.experimental.pallas import tpu as pltpu
from jax.sharding import Mesh
from jax.sharding import PartitionSpec as P


PLANE = ("x", "y", "core")
DEPTH = ("zl", "zh")
EPSILON = 1e-05
BF = jnp.bfloat16
F32 = jnp.float32


def dot(a, b, dims=((1,), (0,))):
    return lax.dot_general(a, b, (dims, ((), ())), preferred_element_type=F32)


def norm(values):
    center = jnp.mean(values, axis=0, keepdims=True)
    shifted = values - center
    inverse = lax.rsqrt(jnp.mean(shifted * shifted, axis=0, keepdims=True) + EPSILON)
    return shifted * inverse, inverse


def norm_back(weighted, scaled, inverse):
    first = jnp.mean(weighted, axis=0, keepdims=True)
    second = jnp.mean(weighted * scaled, axis=0, keepdims=True)
    return inverse * (weighted - first - scaled * second)


def pair_order():
    here = lax.broadcasted_iota(jnp.int32, (128, 128), 0)
    there = lax.broadcasted_iota(jnp.int32, (128, 128), 1)
    same = (here >> 3 == (there & 15)) & ((here & 7) == there >> 4)
    return same.astype(F32).astype(BF)


def column(gain):
    return jnp.broadcast_to(gain, (128, 128)).T


def groups(values):
    return values.reshape(16, 8, 128).astype(BF)


def take(got, array):
    return got[:, 8 * array : 8 * array + 8].astype(F32).reshape(128, 128)


def swap_groups(rows):
    rows = list(rows)
    group = lax.broadcasted_iota(jnp.int32, rows[0].shape, 1) >> 4
    step = len(rows) // 2
    while step:
        low = (group & step) == 0
        for a in range(len(rows)):
            if a & step:
                continue
            x, y = rows[a], rows[a + step]
            rows[a] = jnp.where(low, x, pltpu.roll(y, 16 * step, 1))
            rows[a + step] = jnp.where(low, pltpu.roll(x, 128 - 16 * step, 1), y)
        step //= 2
    return rows


def spread_kernel(full, parts, got, send, held_full, held_parts):
    pieces = []
    for high in range(2):
        rows = swap_groups(
            [got[4 * zl + 2 * high + low].astype(F32) for low in range(2) for zl in range(4)]
        )
        for q in range(8):
            held_full[:, 8 * high + q] = rows[q][8 * full : 8 * full + 8]
            pieces.append([rows[q][8 * a : 8 * a + 8] for a in parts])
    if len(parts) == 1:
        pieces = [pieces[q] + pieces[8 + q] for q in range(8)]
    for row, arrays in enumerate(pieces):
        for mate, values in enumerate(swap_groups(arrays + arrays[: 4 - len(arrays)])):
            held_parts[:, mate, row] = values
    values = held_full[...].astype(BF)
    for mate in range(4):
        send[:, mate, 0:16] = values
    send[:, :, 16:] = held_parts[...].astype(BF)


def collect_kernel(full, parts, got, send, held, held_parts, out):
    values = got[...].astype(F32)
    held[...] = values[:, 0, 0:16] + values[:, 1, 0:16] + values[:, 2, 0:16] + values[:, 3, 0:16]
    held_parts[...] = values[:, :, 16:]
    pieces = [
        swap_groups([held_parts[:, mate, row] for mate in range(4)])
        for row in range(got.shape[2] - 16)
    ]
    if len(parts) == 1:
        pieces = [[values[high]] for high in range(2) for values in pieces]
    for high in range(2):
        arrays = {full: [held[:, 8 * high + q] for q in range(8)]}
        for n, a in enumerate(parts):
            arrays[a] = [pieces[8 * high + q][n] for q in range(8)]
        for a, rows in arrays.items():
            for g, values in enumerate(swap_groups(rows)):
                zh = 2 * high + (g >> 2)
                out[4 * (g & 3) + zh, 8 * a : 8 * a + 8] = values
    send[...] = out[...].astype(BF)


def swap_halves(first, second):
    low = lax.broadcasted_iota(jnp.int32, first.shape, 1) < 64
    return (
        jnp.where(low, first, pltpu.roll(second, 64, 1)),
        jnp.where(low, pltpu.roll(first, 64, 1), second),
    )


def whole(got, big):
    tiles = [got[x, :, 0:16].astype(F32).reshape(128, 128) for x in range(4)]
    left = swap_halves(tiles[0], tiles[1])
    right = swap_halves(tiles[2], tiles[3])
    values = jnp.concatenate(
        [jnp.concatenate([left[low], right[low]], axis=1) for low in range(2)], axis=0
    )
    return dot(values.astype(BF), big[0:256])


def quarters(got):
    rows = got.shape[2] - 16
    tiles = [got[x, :, 16:].astype(F32).reshape(8 * rows, 128) for x in range(4)]
    arrays = swap_groups(tiles)
    if rows == 8:
        highs = [values.reshape(8, 1, 8, 128) for values in arrays[:2]]
        arrays = [jnp.concatenate(highs, axis=1).reshape(128, 128)]
    turned = [values.T for values in arrays[:3]]
    return [jnp.concatenate([t[0:64], t[64:128]], axis=1).astype(BF) for t in turned]


def send_whole(send, values, big):
    values = dot(values.astype(BF), big[256:512])
    for half in range(2):
        lanes = slice(128 * half, 128 * half + 128)
        tiles = swap_halves(values[0:128, lanes], values[128:256, lanes])
        for n in range(2):
            send[2 * half + n, :, 0:16] = tiles[n].reshape(8, 16, 128).astype(BF)


def send_quarters(send, arrays):
    rows = [
        jnp.concatenate([values[:, 0:128], values[:, 128:256]], axis=0).T for values in arrays
    ]
    if len(rows) == 1:
        highs = rows[0].reshape(8, 2, 8, 128)
        rows = [highs[:, n].reshape(64, 128) for n in range(2)]
    rows += rows[: 4 - len(rows)]
    for x, tile in enumerate(swap_groups(rows)):
        send[x, :, 16:] = tile.reshape(8, send.shape[2] - 16, 128).astype(BF)


def join(pieces):
    return jnp.concatenate(pieces, axis=0)


NN = ((1,), (0,))
NT = ((1,), (1,))
TN = ((0,), (0,))


def q_block(place):
    return ((place >> 5) & 3) * 4 + ((place >> 3) & 1) * 2 + (place >> 7)


def tables():
    place = np.arange(256)
    residue_p = (((place >> 4) & 3) * 4 + (place >> 6)) * 16 + (place & 15)
    residue_q = q_block(place) * 16 + ((place >> 4) & 1) * 8 + (place & 7)
    order = residue_p[:, None] == residue_q[None, :]
    blocks = q_block(place)[:, None] == place[None, :] >> 4
    long = q_block(place)[:, None] == np.arange(16)[None, :]
    wide = q_block(place)[::8, None] == (place & 15)[None, :]
    big = np.concatenate([order, order.T], axis=0)
    small = np.concatenate([long, long[::8]], axis=0)
    big, blocks, small = (jnp.asarray(x.astype(ml_dtypes.bfloat16)) for x in (big, blocks, small))
    return big, blocks, small, jnp.asarray(wide.astype(np.float32))


def masks(contact, flat, mate, blocks, small, wide):
    by_k = flat[...].astype(F32)
    wanted = lax.broadcasted_iota(jnp.int32, (4, 16), 0) + 4 * mate
    label = lax.broadcasted_iota(jnp.int32, (4, 16), 1)
    by_k = dot((label == wanted).astype(F32).astype(BF), by_k.astype(BF), NT)
    short, long = small[256:288], small[0:256]
    for_out = [
        dot(short, contact[4 * mate + t].astype(F32).astype(BF), NT).astype(BF) for t in range(4)
    ]
    for_in = [(wide[...] * by_k[t : t + 1]).astype(BF) for t in range(4)]
    return dot(join(for_out), long, NT), dot(join(for_in), blocks[...], NT)


def apply(masks, t, values):
    mask = masks[32 * t : 32 * t + 32].reshape(32, 1, 256)
    return (values.reshape(32, 8, 256) * mask).reshape(256, 256)


def forward_kernel(got, made, big, send, kept):
    left_out, left_in, right_in = quarters(got)
    right_out = whole(got, big)
    for n, values in enumerate((left_out, left_in, right_in)):
        kept[64 * n : 64 * n + 64] = values
    kept[192:448] = right_out.astype(BF)
    mask_out, mask_in = made[0:128].astype(F32), made[128:256].astype(F32)
    outs, ins = [], None
    for t in range(4):
        part = slice(16 * t, 16 * t + 16)
        outs.append(dot(left_out[part], apply(mask_out, t, right_out).astype(BF), NN))
        term = apply(mask_in, t, dot(right_in[part], left_in[part], TN))
        ins = term if ins is None else ins + term
    send_whole(send, ins, big)
    send_quarters(send, [join(outs)])


def backward_kernel(kept, grads, made, big, send):
    left_out, left_in, right_in = (kept[64 * n : 64 * n + 64] for n in range(3))
    grad_out = quarters(grads)[0]
    right_out = kept[192:448].astype(F32)
    grad_in = whole(grads, big)
    mask_out, mask_in = made[0:128].astype(F32), made[128:256].astype(F32)
    grad_left_out, grad_left_in, grad_right_in, grad_right_out = [], [], [], None
    for t in range(4):
        part = slice(16 * t, 16 * t + 16)
        over_j = apply(mask_out, t, right_out).astype(BF)
        grad_left_out.append(dot(grad_out[part], over_j, NT))
        term = apply(mask_out, t, dot(left_out[part], grad_out[part], TN))
        grad_right_out = term if grad_right_out is None else grad_right_out + term
        both = apply(mask_in, t, grad_in).astype(BF)
        grad_left_in.append(dot(right_in[part], both, NN))
        grad_right_in.append(dot(left_in[part], both, NT))
    send_whole(send, grad_right_out, big)
    send_quarters(send, [join(grad_left_out), join(grad_left_in), join(grad_right_in)])


def first_kernel(
    spot, pair, gain, w_out, w_in, update, contact, flat, blocks, small, wide, send, rest, made, proj
):
    scaled, inverse = norm(dot(pair[...], pair_order(), ((0,), (0,))))
    normed = (scaled * column(gain[...])).astype(BF)
    rest[0:128] = scaled
    rest[128:129] = inverse
    rest[129:130] = gain[...]
    for half, weights in enumerate((w_out, w_in)):
        p = dot(weights[...], normed, ((0,), (0,)))
        proj[half] = p
        for side in range(2):
            part = 256 * side
            gated = jax.nn.sigmoid(p[part : part + 128]) * p[part + 128 : part + 256]
            row = 16 * half + 8 * side
            send[:, row : row + 8] = groups(gated)
    rest[130:132] = update[...]
    mask_out, mask_in = masks(contact, flat, spot[0], blocks, small, wide)
    made[0:128] = mask_out.astype(BF)
    made[128:256] = mask_in.astype(BF)


def middle_kernel(pair, cotangent, got, rest, w_gate, w_final, final, send, grad_gate):
    order = pair_order()
    upstream = dot(cotangent[...], order, TN)
    total = dot(pair[...], order, TN)
    normed_pair = (rest[0:128] * column(rest[129:130])).astype(BF)
    gates = jax.nn.sigmoid(dot(w_gate[...], normed_pair, TN))
    for t in range(2):
        scaled, inverse = norm(take(got, t))
        gain_t = column(rest[130 + t : 131 + t])
        normed = (scaled * gain_t).astype(BF)
        gate = gates[128 * t : 128 * t + 128]
        product = dot(w_final[t], normed, TN)
        total = total + gate * product
        grad_final = (upstream * gate).astype(BF)
        grad_gate[128 * t : 128 * t + 128] = (upstream * product * gate * (1.0 - gate)).astype(BF)
        weighted = dot(w_final[t], grad_final) * gain_t
        send[:, 8 * t : 8 * t + 8] = groups(norm_back(weighted, scaled, inverse))
    final[...] = total.astype(BF)


def last_kernel(
    cotangent, got, grad_gate, rest, proj, final, w_out, w_in, w_gate, updated, grad_pair
):
    order = pair_order()
    upstream = dot(cotangent[...], order, TN)
    updated[...] = dot(order, final[...], NT).astype(BF)
    grad_normed = dot(w_gate[...], grad_gate[...])
    scaled, inverse, gain = rest[0:128], rest[128:129], column(rest[129:130])
    for half, weights in enumerate((w_out, w_in)):
        p = proj[half]
        parts = []
        for side in range(2):
            grad = take(got, 2 * half + side)
            sig = jax.nn.sigmoid(p[256 * side : 256 * side + 128])
            parts.append(grad * p[256 * side + 128 : 256 * side + 256] * sig * (1.0 - sig))
            parts.append(grad * sig)
        grad_normed = grad_normed + dot(
            weights[...], jnp.concatenate(parts, axis=0).astype(BF)
        )
    back = norm_back(grad_normed * gain, scaled, inverse)
    grad_pair[...] = dot(order, (upstream + back).astype(BF), NT).astype(BF)


def call(kernel, out, *args, scratch=(), spot=False, limit=32 * 1024 * 1024):
    specs = [pl.BlockSpec(memory_space=pltpu.VMEM)] * len(args)
    if spot:
        specs[0] = pl.BlockSpec(memory_space=pltpu.SMEM)
    multi = isinstance(out, list)
    shapes = [jax.ShapeDtypeStruct(s, d) for s, d in (out if multi else [out])]
    outs = [pl.BlockSpec(memory_space=pltpu.VMEM)] * len(shapes)
    params = pltpu.CompilerParams(vmem_limit_bytes=limit) if limit else None
    result = pl.pallas_call(
        kernel,
        out_shape=shapes,
        in_specs=specs,
        out_specs=outs,
        scratch_shapes=[pltpu.VMEM(s, F32) for s in scratch],
        compiler_params=params,
    )(*args)
    return result if multi else result[0]


def exchange(values, axis):
    return lax.all_to_all(values, axis, 0, 0, tiled=True)


def to_channels(send, full, parts):
    rows = 24 if len(parts) == 1 else 32
    spread = call(
        functools.partial(spread_kernel, full, parts),
        ((8, 4, rows, 128), BF),
        exchange(send, DEPTH),
        scratch=[(8, 16, 128), (8, 4, rows - 16, 128)],
    )
    return exchange(spread.reshape(32, rows, 128), PLANE).reshape(4, 8, rows, 128)


def to_pairs(send, full, parts):
    rows = send.shape[2]
    amount = 8 + 8 * len(parts)
    back = call(
        functools.partial(collect_kernel, full, parts),
        ((16, amount, 128), BF),
        exchange(send.reshape(32, rows, 128), PLANE).reshape(8, 4, rows, 128),
        scratch=[(8, 16, 128), (8, 4, rows - 16, 128), (16, amount, 128)],
    )
    return exchange(back, DEPTH)


def my_mate():
    return lax.axis_index(PLANE) & 3


def on_device(
    pair_rep, cotangent, contact, norm_gain, w_out_proj, w_in_proj, update_gain, w_gate, w_final
):
    pair = pair_rep.reshape(128, 128)
    upstream = cotangent.reshape(128, 128)
    flat = contact.reshape(256, 16)

    big, blocks, small, wide = tables()
    send, rest, made, proj = call(
        first_kernel,
        [
            ((16, 32, 128), BF),
            ((136, 128), F32),
            ((256, 256), BF),
            ((2, 512, 128), F32),
        ],
        my_mate().reshape(1),
        pair,
        norm_gain.reshape(1, 128),
        w_out_proj,
        w_in_proj,
        update_gain,
        contact,
        flat,
        blocks,
        small,
        wide,
        spot=True,
        limit=None,
    )
    sides = to_channels(send, 1, (0, 2, 3))
    triangles, kept = call(
        forward_kernel, [((4, 8, 24, 128), BF), ((448, 256), BF)], sides, made, big
    )
    final, send, grad_gate = call(
        middle_kernel,
        [((128, 128), BF), ((16, 16, 128), BF), ((256, 128), BF)],
        pair,
        upstream,
        to_pairs(triangles, 1, (0,)),
        rest,
        w_gate,
        w_final,
    )
    grads = call(
        backward_kernel,
        ((4, 8, 32, 128), BF),
        kept,
        to_channels(send, 1, (0,)),
        made,
        big,
    )
    updated, grad_pair = call(
        last_kernel,
        [((128, 128), BF), ((128, 128), BF)],
        upstream,
        to_pairs(grads, 1, (0, 2, 3)),
        grad_gate,
        rest,
        proj,
        final,
        w_out_proj,
        w_in_proj,
        w_gate,
    )
    return (updated.reshape(pair_rep.shape), grad_pair.reshape(pair_rep.shape))


def solution(mesh):
    fine = Mesh(mesh.devices.reshape(4, 4, 4, 4, 2), ("zl", "x", "y", "zh", "core"))
    block = P(("zl", "x"), ("y", "zh", "core"), None)
    in_specs = (block, block, P(), P(), P(), P(), P(), P(), P())
    return jax.shard_map(
        on_device, mesh=fine, in_specs=in_specs, out_specs=(block, block), check_vma=False
    )
```
